32 devices in a mesh: dst: 8 (over z, y), src: 4 (over x, core).
Axes of the slice: x: 2, y: 2, z: 4, core: 2. Of those that a mesh axis runs over, the one named last changes fastest.
Arguments:
- transitions: bfloat16 [2048, 128, 128], P(('dst', 'src')), may hold values from 0.0009994507 to 1
- row_block: int32 [2048], P(('dst', 'src')), may hold values from -1 to 1023, as said below
- col_block: int32 [2048], P(('dst', 'src')), may hold values from -1 to 1023, as said below
- beta_last: float32 [32, 256, 4, 128], P(None, 'dst', 'src'), may hold values from 0.2 to 2
- emissions: bfloat16 [2, 32, 256, 4, 128], P(None, None, 'dst', 'src'), may hold values from 0.019897461 to 1
- forward: bfloat16 [2, 32, 256, 4, 128], P(None, None, 'dst', 'src'), may hold values from 0.03 to 125, as said below
Outputs:
- counts: bfloat16 [2048, 128, 128], P(('dst', 'src'))
- beta_first: float32 [32, 256, 4, 128], P(None, 'dst', 'src')
- log_norms: float32 [2, 32], replicated
The draws below stay inside these ranges and needn't reach their ends.
Inputs may be any that keep to these rules, and one draw needn't show every extreme that they name: `row_block`: slots are grouped by device (index dst * 4 + src), 64 to a device. A live slot holds a block whose source block number r has r % 4 equal to the device's src index and whose destination block lies in the device's dst index's own consecutive equal share of blocks; no block appears twice; live slots come first, and empty ones hold -1 in both arrays. One device has all 64 slots live; each device has at least one. `col_block`: same slots as row_block; -1 exactly where row_block is -1. `forward`: Positive.
All inputs are finite; a program needn't handle non-finite values.
Results may differ from the reference program's by a relative error of at most 0.0029.
Values may be sent and summed in bfloat16 or wider, within the bound.
A program may use at most 64 MiB of HBM per device.

```python
import math
import jax
import jax.numpy as jnp
from jax import lax

S = 131072
BLK = 128
B = 32
CAP = 64
STEPS = 2
ROW_SPAN = 256
SLOTS = 2048
N_DST = 8
N_SRC = 4


def pick_slots(sub_key, candidates):
    return jax.random.permutation(sub_key, candidates)[:CAP].astype(jnp.int32)


def pattern(key):
    tile_total = N_DST * N_SRC
    row_span = S // (BLK * N_SRC)
    col_span = S // (BLK * N_DST)
    key_count, key_busy, key_perm = jax.random.split(jax.random.fold_in(key, 7), 3)
    filled = jax.random.randint(key_count, (tile_total,), 1, CAP + 1).astype(jnp.int32)
    busiest = jax.random.randint(key_busy, (), 0, tile_total).astype(jnp.int32)
    tile_ids = jnp.arange(tile_total, dtype=jnp.int32)
    filled = jnp.where(tile_ids == busiest, CAP, filled)
    sub_keys = jax.random.split(key_perm, tile_total)
    chosen = jax.vmap(lambda sub_key: pick_slots(sub_key, row_span * col_span))(sub_keys)
    row_ids = chosen // col_span * N_SRC + (tile_ids % N_SRC)[:, None]
    col_ids = (tile_ids // N_SRC)[:, None] * col_span + chosen % col_span
    living = jnp.arange(CAP, dtype=jnp.int32)[None, :] < filled[:, None]
    row_out = jnp.where(living, row_ids, -1).reshape(-1).astype(jnp.int32)
    col_out = jnp.where(living, col_ids, -1).reshape(-1).astype(jnp.int32)
    return (row_out, col_out)


def draw_row_block(key, part):
    return pattern(key)[0]


def draw_col_block(key, part):
    return pattern(key)[1]


def draw_forward(key, part):
    row_span = S // (BLK * N_SRC)
    key_state, key_seq, key_rough = jax.random.split(jax.random.fold_in(key, 11), 3)
    position = jnp.arange(S, dtype=jnp.float32).reshape(1, 1, row_span, N_SRC, BLK)
    ramped = 1.0 + 2.0 * position / S
    state_scale = jnp.exp(jax.random.uniform(key_state, (1, 1, row_span, N_SRC, BLK), jnp.float32, 0.0, math.log(10.0)))
    seq_scale = jnp.exp(jax.random.uniform(key_seq, (1, B, 1, 1, 1), jnp.float32, 0.0, math.log(10.0)))
    rough = jnp.exp(jax.random.uniform(key_rough, (STEPS, B, row_span, N_SRC, BLK), jnp.float32, -0.9, 0.9))
    return (0.1 * ramped * state_scale * seq_scale * rough).astype(jnp.bfloat16)


def levels(own_key, dims, cuts, smallest, top_value):
    loudness, own = 1.0, jax.random.fold_in(own_key, 6)
    for dim, blocks in cuts:
        heights = jnp.exp(jax.random.uniform(jax.random.fold_in(own, dim), (blocks,), jnp.float32, smallest / len(cuts), top_value / len(cuts)))
        loudness = loudness * jnp.repeat(heights, dims[dim] // blocks).reshape([-1 if axis == dim else 1 for axis in range(len(dims))])
    return loudness


def setup_inputs(seed: int = 0) -> dict:
    keys = jax.random.split(jax.random.key(seed), 7)
    return {
        "transitions": jnp.clip(jnp.exp(math.log(1.0) - 6.9083047 * jax.random.uniform(keys[0], (SLOTS, BLK, BLK), jnp.float32) ** levels(keys[0], (SLOTS, BLK, BLK), ((0, 32),), -0.2, 0.2)), 0.0009994507, 1.0).astype(jnp.bfloat16),
        "row_block": draw_row_block(jax.random.fold_in(keys[6], 71), 0),
        "col_block": draw_col_block(jax.random.fold_in(keys[6], 71), 0),
        "beta_last": jnp.clip(jnp.exp(math.log(2.0) - 2.3025851 * jax.random.uniform(keys[3], (B, ROW_SPAN, N_SRC, BLK), jnp.float32) ** levels(keys[3], (B, ROW_SPAN, N_SRC, BLK), ((1, 8), (2, 4)), -0.2, 0.2)), 0.2, 2.0),
        "emissions": jnp.clip(jnp.exp(math.log(1.0) - 3.9171631 * jax.random.uniform(keys[4], (STEPS, B, ROW_SPAN, N_SRC, BLK), jnp.float32) ** levels(keys[4], (STEPS, B, ROW_SPAN, N_SRC, BLK), ((2, 8), (3, 4)), -0.2, 0.2)), 0.019897461, 1.0).astype(jnp.bfloat16),
        "forward": draw_forward(jax.random.fold_in(keys[6], 71), 0),
    }


def reference(transitions, row_block, col_block, beta_last, emissions, forward):
    tile_total = N_DST * N_SRC
    slot_blocks = transitions.reshape(tile_total, CAP, BLK, BLK)
    rows_all = row_block.reshape(tile_total, CAP)
    cols_all = col_block.reshape(tile_total, CAP)
    total_blocks = S // BLK
    seq_count = beta_last.shape[0]
    beta_now = beta_last.reshape(seq_count, total_blocks, BLK)
    alpha_list = []
    scaled_list = []
    log_list = []
    for step_index in range(STEPS):
        emitted = emissions[step_index].reshape(seq_count, total_blocks, BLK)
        message = (emitted.astype(jnp.float32) * beta_now).astype(jnp.bfloat16)
        message_blocks = jnp.transpose(message, (1, 0, 2))

        def one_tile(running, tile_data):
            trans_tile, rows_tile, cols_tile = tile_data
            living = rows_tile >= 0
            cols_safe = jnp.where(living, cols_tile, 0).astype(jnp.int32)
            rows_safe = jnp.where(living, rows_tile, 0).astype(jnp.int32)
            picked = message_blocks[cols_safe].astype(jnp.float32)
            products = jnp.einsum("cbj,cij->cbi", picked, trans_tile.astype(jnp.float32))
            products = products * living.astype(jnp.float32)[:, None, None]
            return running.at[rows_safe].add(products), None

        start = jnp.zeros((total_blocks, seq_count, BLK), jnp.float32)
        raw_sums = lax.scan(one_tile, start, (slot_blocks, rows_all, cols_all))[0]
        alpha_blocks = jnp.transpose(forward[step_index].reshape(seq_count, total_blocks, BLK), (1, 0, 2))
        scale_now = jnp.sum(alpha_blocks.astype(jnp.float32) * raw_sums, axis=(0, 2)) / S
        beta_now = jnp.transpose(raw_sums / scale_now[None, :, None], (1, 0, 2))
        scaled = (message_blocks.astype(jnp.float32) / scale_now[None, :, None]).astype(jnp.bfloat16)
        alpha_list.append(alpha_blocks)
        scaled_list.append(scaled)
        log_list.append(jnp.log(scale_now))
    alpha_stack = jnp.stack(alpha_list)
    scaled_stack = jnp.stack(scaled_list)

    def tile_counts(tile_data):
        trans_tile, rows_tile, cols_tile = tile_data
        living = rows_tile >= 0
        cols_safe = jnp.where(living, cols_tile, 0).astype(jnp.int32)
        rows_safe = jnp.where(living, rows_tile, 0).astype(jnp.int32)
        alpha_picked = alpha_stack[:, rows_safe].astype(jnp.float32)
        scaled_picked = scaled_stack[:, cols_safe].astype(jnp.float32)
        count_sum = jnp.einsum("tcbi,tcbj->cij", alpha_picked, scaled_picked)
        masked = count_sum * trans_tile.astype(jnp.float32) * living.astype(jnp.float32)[:, None, None]
        return masked.astype(jnp.bfloat16)

    counts = lax.map(tile_counts, (slot_blocks, rows_all, cols_all)).reshape(tile_total * CAP, BLK, BLK)
    beta_first = beta_now.reshape(seq_count, total_blocks // N_SRC, N_SRC, BLK)
    return counts, beta_first, jnp.stack(log_list)
```

```python
import functools

import jax
import jax.numpy as jnp
from jax import lax
from jax.experimental import pallas as pl
from jax.experimental.pallas import tpu as pltpu
from jax.sharding import PartitionSpec as P

MESH = pl.DeviceIdType.MESH


def kernel(nd, ns, total_states, table,
           trans, msg0, em1, fwd, counts, beta, scales,
           msgs0, msgs1, fwds0, fwds1, run, parts, ypart, zsend, zpart, tdst, tsrc,
           send_m, recv_m, send_f, recv_f, send_y, recv_y, send_z, recv_z,
           send_td, recv_td, send_ts, recv_ts):
    local, seqs, blk = msg0.shape
    slots = trans.shape[0]
    nz, nx = nd // 2, ns // 2
    me_d, me_s = lax.axis_index("dst"), lax.axis_index("src")
    z, y = me_d // 2, me_d % 2
    x, core = me_s // 2, me_s % 2

    def at_dst(d):
        return (d, me_s)

    def at_src(s):
        return (me_d, s)

    def copy(src, dst, ssem, rsem, dev):
        return pltpu.make_async_remote_copy(
            src_ref=src, dst_ref=dst, send_sem=ssem, recv_sem=rsem,
            device_id=dev, device_id_type=MESH)

    barrier = pltpu.get_barrier_semaphore()
    for o in range(1, nd):
        pl.semaphore_signal(barrier, inc=1, device_id=at_dst((me_d + o) % nd), device_id_type=MESH)
    for o in range(1, ns):
        pl.semaphore_signal(barrier, inc=1, device_id=at_src((me_s + o) % ns), device_id_type=MESH)
    pl.semaphore_wait(barrier, nd + ns - 2)

    msgs, fwds = (msgs0, msgs1), (fwds0, fwds1)
    pending = []

    def gather_side(own, buf, k, me, side_dev, ssem, rsem):
        c = copy(own, buf[k].at[me], ssem.at[k, 0], rsem.at[k, me], side_dev)
        c.start()
        pending.append(c)

    def gather_line(own, buf, k, me, count, dev, ssem, rsem):
        pos, side = me // 2, me % 2
        for o in range(1, count):
            c = copy(own, buf[k].at[me], ssem.at[k, o], rsem.at[k, me],
                     dev((pos + o) % count * 2 + side))
            c.start()
            pending.append(c)

    def gather_pass(buf, k, me, count, side_dev, ssem, rsem):
        pos, side = me // 2, me % 2
        for o in range(1, count):
            e = (pos + count - o) % count * 2 + side
            c = copy(buf[k].at[e], buf[k].at[e], ssem.at[k, count + o - 1], rsem.at[k, e], side_dev)
            c.wait_recv()
            c.start()
            pending.append(c)

    def gather_end(buf, k, me, count, side_dev, ssem, rsem):
        pos, side = me // 2, me % 2
        for o in range(count):
            e = (pos + count - o) % count * 2 + 1 - side
            copy(buf[k].at[e], buf[k].at[e], ssem.at[k, 0], rsem.at[k, e], side_dev).wait_recv()

    mate_d = at_dst(z * 2 + 1 - y)
    mate_s = at_src(x * 2 + 1 - core)

    def message_gather(k):
        own = msgs[k].at[me_s]
        gather_line(own, msgs, k, me_s, nx, at_src, send_m, recv_m)
        gather_side(own, msgs, k, me_s, mate_s, send_m, recv_m)

    def message_arrive(k):
        gather_pass(msgs, k, me_s, nx, mate_s, send_m, recv_m)
        gather_end(msgs, k, me_s, nx, mate_s, send_m, recv_m)

    def products(k):
        run[0] = jnp.zeros((seqs, blk), jnp.float32)

        def one(j, carry):
            c = table[slots + j]
            block = msgs[k][c // local, c % local]
            run[j + 1] = lax.dot_general(block, trans[table[j]], (((1,), (1,)), ((), ())),
                                         preferred_element_type=jnp.float32)
            return carry

        lax.fori_loop(0, slots, one, 0, unroll=8)

        def add_run(j, acc):
            acc = run[j + 1] + acc * table[2 * slots + j].astype(jnp.float32)
            run[j + 1] = acc
            return acc

        lax.fori_loop(0, slots, add_run, jnp.zeros((seqs, blk), jnp.float32), unroll=4)

        for d in range(nd):
            def put(a, carry, d=d):
                parts[k, d, a] = run[table[6 * slots + d * local + a]].astype(jnp.bfloat16)
                return carry

            lax.fori_loop(0, local, put, 0, unroll=4)

    def reduce_side(k):
        for o in range(1, nz + 1):
            zt = (z + o) % nz
            c = copy(parts.at[k, zt * 2 + 1 - y], ypart.at[k, zt], send_y.at[k, o - 1],
                     recv_y.at[k, zt], mate_d)
            c.start()
            pending.append(c)

    def reduce_line(k):
        for o in range(1, nz):
            zt = (z + o) % nz
            copy(parts.at[k, zt * 2 + 1 - y], ypart.at[k, zt], send_y.at[k, o - 1],
                 recv_y.at[k, zt], mate_d).wait_recv()

            def add(a, carry):
                zsend[k, zt, a] = (parts[k, zt * 2 + y, a].astype(jnp.float32)
                                   + ypart[k, zt, a].astype(jnp.float32)).astype(jnp.bfloat16)
                return carry

            lax.fori_loop(0, local, add, 0, unroll=4)
            c = copy(zsend.at[k, zt], zpart.at[k, z], send_z.at[k, o - 1], recv_z.at[k, z],
                     at_dst(zt * 2 + y))
            c.start()
            pending.append(c)

    def reduce_end(k):
        copy(parts.at[k, z * 2 + 1 - y], ypart.at[k, z], send_y.at[k, nz - 1],
             recv_y.at[k, z], mate_d).wait_recv()
        for o in range(1, nz):
            zf = (z + nz - o) % nz
            copy(zsend.at[k, zf], zpart.at[k, zf], send_z.at[k, o - 1], recv_z.at[k, zf],
                 mate_d).wait_recv()

        def add(a, total):
            raw = parts[k, me_d, a].astype(jnp.float32) + ypart[k, z, a].astype(jnp.float32)
            for o in range(1, nz):
                raw = raw + zpart[k, (z + nz - o) % nz, a].astype(jnp.float32)
            beta[a] = raw
            if k == 0:
                msgs[1][me_s, a] = (em1[a].astype(jnp.float32) * raw).astype(jnp.bfloat16)
            return total + fwd[k, a].astype(jnp.float32) * raw

        total = lax.fori_loop(0, local, add, jnp.zeros((seqs, blk), jnp.float32), unroll=2)
        tdst[me_d, pl.ds(k * seqs, seqs)] = total

    def keep_message(a, carry):
        msgs[0][me_s, a] = msg0[a]
        return carry

    lax.fori_loop(0, local, keep_message, 0, unroll=4)
    message_gather(0)
    for k in range(2):
        def keep_forward(a, carry, k=k):
            fwds[k][me_d, a] = fwd[k, a]
            return carry

        lax.fori_loop(0, local, keep_forward, 0, unroll=4)
        gather_side(fwds[k].at[me_d], fwds, k, me_d, mate_d, send_f, recv_f)
    gather_line(fwds[0].at[me_d], fwds, 0, me_d, nz, at_dst, send_f, recv_f)
    message_arrive(0)
    products(0)
    reduce_side(0)
    reduce_line(0)
    gather_pass(fwds, 0, me_d, nz, mate_d, send_f, recv_f)
    gather_line(fwds[1].at[me_d], fwds, 1, me_d, nz, at_dst, send_f, recv_f)
    reduce_end(0)

    message_gather(1)
    message_arrive(1)
    products(1)
    reduce_side(1)
    reduce_line(1)
    gather_pass(fwds, 1, me_d, nz, mate_d, send_f, recv_f)
    reduce_end(1)

    for o in range(1, nd):
        c = copy(tdst.at[me_d], tdst.at[me_d], send_td.at[o - 1], recv_td.at[me_d],
                 at_dst((me_d + o) % nd))
        c.start()
        pending.append(c)
    for o in range(1, nd):
        e = (me_d + o) % nd
        copy(tdst.at[e], tdst.at[e], send_td.at[o - 1], recv_td.at[e], at_dst(e)).wait_recv()
    tsrc[me_s] = sum(tdst[d] for d in range(nd))
    for o in range(1, ns):
        c = copy(tsrc.at[me_s], tsrc.at[me_s], send_ts.at[o - 1], recv_ts.at[me_s],
                 at_src((me_s + o) % ns))
        c.start()
        pending.append(c)
    for o in range(1, ns):
        e = (me_s + o) % ns
        copy(tsrc.at[e], tsrc.at[e], send_ts.at[o - 1], recv_ts.at[e], at_src(e)).wait_recv()
    whole = sum(tsrc[s] for s in range(ns))
    norm = jnp.sum(whole, axis=1, keepdims=True) / total_states
    norm = jnp.broadcast_to(norm, (2 * seqs, blk))
    scales[...] = norm
    inverse = 1.0 / norm

    def finish(a, carry):
        beta[a] = beta[a] / norm[seqs:]
        return carry

    lax.fori_loop(0, local, finish, 0)

    for k in range(2):
        gather_end(fwds, k, me_d, nz, mate_d, send_f, recv_f)

    def count(m, carry):
        r, c = table[3 * slots + m], table[4 * slots + m]
        left = jnp.concatenate([fwds[k][r // local, r % local] for k in range(2)], axis=0)
        right = jnp.concatenate([msgs[k][c // local, c % local] for k in range(2)], axis=0)
        right = (right.astype(jnp.float32) * inverse).astype(jnp.bfloat16)
        value = lax.dot_general(left, right, (((0,), (0,)), ((), ())),
                                preferred_element_type=jnp.float32)
        counts[m] = (value * trans[m].astype(jnp.float32) * table[5 * slots + m].astype(jnp.float32)).astype(jnp.bfloat16)
        return carry

    lax.fori_loop(0, slots, count, 0, unroll=4)
    for c in pending:
        c.wait_send()


def body(nd, ns, transitions, row_block, col_block, beta_last, emissions, forward):
    seqs, local, _, blk = beta_last.shape
    slots = transitions.shape[0]
    columns, rows = local * ns, local * nd
    total_states = rows * ns * blk

    live = row_block >= 0
    row = jnp.where(live, row_block // ns, 0)
    col = jnp.where(live, col_block % columns, 0)
    col = col % ns * local + col // ns
    key = jnp.where(live, row, rows)
    number = jnp.arange(slots)
    before = (key[None, :] < key[:, None]) | (
        (key[None, :] == key[:, None]) & (number[None, :] < number[:, None]))
    rank = jnp.sum(before.astype(jnp.int32), axis=1)
    place = (rank[None, :] == number[:, None]).astype(jnp.int32)
    perm = jnp.sum(place * number[None, :].astype(jnp.int32), axis=1)
    pcol = jnp.sum(place * col[None, :], axis=1)
    same = jnp.any((key[None, :] == key[:, None]) & (rank[None, :] == rank[:, None] - 1), axis=1)
    flag = jnp.sum(place * same[None, :].astype(jnp.int32), axis=1)
    every = jnp.arange(rows)
    last = jnp.where(jnp.any(key[None, :] == every[:, None], axis=1),
                     jnp.sum((key[None, :] <= every[:, None]).astype(jnp.int32), axis=1), 0)

    table = jnp.concatenate(
        [perm, pcol, flag, row, col, live.astype(jnp.int32), last]).astype(jnp.int32)

    def by_block(array):
        return jnp.swapaxes(array[..., 0, :], -3, -2)

    msg0 = by_block((emissions[0].astype(jnp.float32) * beta_last).astype(jnp.bfloat16))
    em1 = by_block(emissions[1])
    fwd = by_block(forward)

    smem = pl.BlockSpec(memory_space=pltpu.SMEM)
    vmem = pl.BlockSpec(memory_space=pltpu.VMEM)
    nz, nx = nd // 2, ns // 2
    block = (local, seqs, blk)
    dma = pltpu.SemaphoreType.DMA
    counts, beta, scales = pl.pallas_call(
        functools.partial(kernel, nd, ns, float(total_states)),
        out_shape=(
            jax.ShapeDtypeStruct(transitions.shape, jnp.bfloat16),
            jax.ShapeDtypeStruct(block, jnp.float32),
            jax.ShapeDtypeStruct((2 * seqs, blk), jnp.float32),
        ),
        in_specs=[smem] + [vmem] * 4,
        out_specs=(vmem, vmem, vmem),
        scratch_shapes=[
            pltpu.VMEM((ns,) + block, jnp.bfloat16),
            pltpu.VMEM((ns,) + block, jnp.bfloat16),
            pltpu.VMEM((nd,) + block, jnp.bfloat16),
            pltpu.VMEM((nd,) + block, jnp.bfloat16),
            pltpu.VMEM((slots + 1, seqs, blk), jnp.float32),
            pltpu.VMEM((2, nd) + block, jnp.bfloat16),
            pltpu.VMEM((2, nz) + block, jnp.bfloat16),
            pltpu.VMEM((2, nz) + block, jnp.bfloat16),
            pltpu.VMEM((2, nz) + block, jnp.bfloat16),
            pltpu.VMEM((nd, 2 * seqs, blk), jnp.float32),
            pltpu.VMEM((ns, 2 * seqs, blk), jnp.float32),
            dma((2, 2 * nx)), dma((2, ns)),
            dma((2, 2 * nz)), dma((2, nd)),
            dma((2, nz)), dma((2, nz)),
            dma((2, nz)), dma((2, nz)),
            dma((nd,)), dma((nd,)),
            dma((ns,)), dma((ns,)),
        ],
        compiler_params=pltpu.CompilerParams(
            collective_id=0, has_side_effects=True, vmem_limit_bytes=48 * 1024 * 1024),
    )(table, transitions, msg0, em1, fwd)
    first, second = scales[:seqs, 0], scales[seqs:, 0]
    logs = jnp.log(jnp.stack([first, second / first]))
    return counts, jnp.swapaxes(beta, 0, 1)[:, :, None, :], logs


def solution(mesh):
    return jax.shard_map(
        functools.partial(body, mesh.shape["dst"], mesh.shape["src"]),
        mesh=mesh,
        in_specs=(
            P(("dst", "src"), None, None),
            P(("dst", "src")),
            P(("dst", "src")),
            P(None, "dst", "src", None),
            P(None, None, "dst", "src", None),
            P(None, None, "dst", "src", None),
        ),
        out_specs=(P(("dst", "src"), None, None), P(None, "dst", "src", None), P()),
        check_vma=False,
    )
```

```python
import functools

import jax
import jax.numpy as jnp
from jax import lax
from jax.experimental import pallas as pl
from jax.experimental.pallas import tpu as pltpu
from jax.sharding import PartitionSpec as P

MESH = pl.DeviceIdType.MESH


def kernel(nd, ns, total_states, table,
           trans, msg0, em1, fwd, counts, beta, scales,
           msgs0, msgs1, fwds0, fwds1, run, parts, ypart, zsend, zpart, tdst, tsrc,
           send_m, recv_m, send_f, recv_f, send_y, recv_y, send_z, recv_z,
           send_td, recv_td, send_ts, recv_ts):
    local, seqs, blk = msg0.shape
    slots = trans.shape[0]
    nz, nx = nd // 2, ns // 2
    me_d, me_s = lax.axis_index("dst"), lax.axis_index("src")
    z, y = me_d // 2, me_d % 2
    x, core = me_s // 2, me_s % 2

    def at_dst(d):
        return (d, me_s)

    def at_src(s):
        return (me_d, s)

    def copy(src, dst, ssem, rsem, dev):
        return pltpu.make_async_remote_copy(
            src_ref=src, dst_ref=dst, send_sem=ssem, recv_sem=rsem,
            device_id=dev, device_id_type=MESH)

    barrier = pltpu.get_barrier_semaphore()
    for o in range(1, nd):
        pl.semaphore_signal(barrier, inc=1, device_id=at_dst((me_d + o) % nd), device_id_type=MESH)
    for o in range(1, ns):
        pl.semaphore_signal(barrier, inc=1, device_id=at_src((me_s + o) % ns), device_id_type=MESH)
    pl.semaphore_wait(barrier, nd + ns - 2)

    msgs, fwds = (msgs0, msgs1), (fwds0, fwds1)
    pending = []

    def other(pos, o):
        for bit in range(o.bit_length()):
            if o >> bit & 1:
                pos = pos + (1 << bit) - 2 * (pos // (1 << bit) % 2) * (1 << bit)
        return pos

    def gather_side(buf, k, me, side_dev, ssem, rsem):
        c = copy(buf[k].at[me], buf[k].at[me], ssem.at[k, 0], rsem.at[k, me], side_dev)
        c.start()
        pending.append(c)

    def gather_line(buf, k, me, count, dev, ssem, rsem):
        pos, side = me // 2, me % 2
        for o in range(1, count):
            c = copy(buf[k].at[me], buf[k].at[me], ssem.at[k, o], rsem.at[k, me],
                     dev(other(pos, o) * 2 + side))
            c.start()
            pending.append(c)

    def gather_pass(buf, k, me, offsets, count, side_dev, ssem, rsem):
        pos, side = me // 2, me % 2
        for o in offsets:
            e = other(pos, o) * 2 + side
            c = copy(buf[k].at[e], buf[k].at[e], ssem.at[k, count + o - 1], rsem.at[k, e], side_dev)
            c.wait_recv()
            c.start()
            pending.append(c)

    def gather_end(buf, k, me, count, side_dev, ssem, rsem):
        pos, side = me // 2, me % 2
        for o in range(count):
            e = other(pos, o) * 2 + 1 - side
            copy(buf[k].at[e], buf[k].at[e], ssem.at[k, 0], rsem.at[k, e], side_dev).wait_recv()

    mate_d = at_dst(z * 2 + 1 - y)
    mate_s = at_src(x * 2 + 1 - core)

    def message_gather(k):
        gather_line(msgs, k, me_s, nx, at_src, send_m, recv_m)
        gather_side(msgs, k, me_s, mate_s, send_m, recv_m)

    def message_arrive(k):
        gather_pass(msgs, k, me_s, range(1, nx), nx, mate_s, send_m, recv_m)
        gather_end(msgs, k, me_s, nx, mate_s, send_m, recv_m)

    def forward_pass(k, offsets):
        gather_pass(fwds, k, me_d, offsets, nz, mate_d, send_f, recv_f)

    def products(k):
        run[0] = jnp.zeros((seqs, blk), jnp.float32)

        def one(j, carry):
            c = table[slots + j]
            block = msgs[k][c // local, c % local]
            run[j + 1] = lax.dot_general(block, trans[table[j]], (((1,), (1,)), ((), ())),
                                         preferred_element_type=jnp.float32)
            return carry

        lax.fori_loop(0, slots, one, 0, unroll=8)

        def add_run(j, acc):
            acc = run[j + 1] + acc * table[2 * slots + j].astype(jnp.float32)
            run[j + 1] = acc
            return acc

        lax.fori_loop(0, slots, add_run, jnp.zeros((seqs, blk), jnp.float32), unroll=4)

        for d in range(nd):
            def put(a, carry, d=d):
                parts[k, d, a] = run[table[6 * slots + d * local + a]].astype(jnp.bfloat16)
                return carry

            lax.fori_loop(0, local, put, 0, unroll=4)

    def reduce_side(k):
        for o in reversed(range(nz)):
            zt = other(z, o)
            c = copy(parts.at[k, zt * 2 + 1 - y], ypart.at[k, zt], send_y.at[k, o],
                     recv_y.at[k, zt], mate_d)
            c.start()
            pending.append(c)

    def reduce_line(k):
        for o in reversed(range(1, nz)):
            zt = other(z, o)
            copy(parts.at[k, zt * 2 + 1 - y], ypart.at[k, zt], send_y.at[k, o],
                 recv_y.at[k, zt], mate_d).wait_recv()

            def add(a, carry):
                zsend[k, zt, a] = (parts[k, zt * 2 + y, a].astype(jnp.float32)
                                   + ypart[k, zt, a].astype(jnp.float32)).astype(jnp.bfloat16)
                return carry

            lax.fori_loop(0, local, add, 0, unroll=4)
            c = copy(zsend.at[k, zt], zpart.at[k, z], send_z.at[k, o - 1], recv_z.at[k, z],
                     at_dst(zt * 2 + y))
            c.start()
            pending.append(c)

    def reduce_end(k):
        copy(parts.at[k, z * 2 + 1 - y], ypart.at[k, z], send_y.at[k, 0],
             recv_y.at[k, z], mate_d).wait_recv()
        for o in range(1, nz):
            zf = other(z, o)
            copy(zsend.at[k, zf], zpart.at[k, zf], send_z.at[k, o - 1], recv_z.at[k, zf],
                 mate_d).wait_recv()

        def add(a, total):
            raw = parts[k, me_d, a].astype(jnp.float32) + ypart[k, z, a].astype(jnp.float32)
            for o in range(1, nz):
                raw = raw + zpart[k, other(z, o), a].astype(jnp.float32)
            beta[a] = raw
            if k == 0:
                msgs[1][me_s, a] = (em1[a].astype(jnp.float32) * raw).astype(jnp.bfloat16)
            return total + fwd[k, a].astype(jnp.float32) * raw

        total = lax.fori_loop(0, local, add, jnp.zeros((seqs, blk), jnp.float32), unroll=2)
        tdst[me_d, pl.ds(k * seqs, seqs)] = total

    def keep_message(a, carry):
        msgs[0][me_s, a] = msg0[a]
        return carry

    lax.fori_loop(0, local, keep_message, 0, unroll=4)
    message_gather(0)
    for k in range(2):
        def keep_forward(a, carry, k=k):
            fwds[k][me_d, a] = fwd[k, a]
            return carry

        lax.fori_loop(0, local, keep_forward, 0, unroll=4)
    gather_line(fwds, 0, me_d, nz, at_dst, send_f, recv_f)
    gather_side(fwds, 0, me_d, mate_d, send_f, recv_f)
    message_arrive(0)
    forward_pass(0, range(1, 2))
    products(0)
    reduce_side(0)
    reduce_line(0)
    forward_pass(0, range(2, nz))
    gather_side(fwds, 1, me_d, mate_d, send_f, recv_f)
    gather_line(fwds, 1, me_d, nz, at_dst, send_f, recv_f)
    reduce_end(0)

    message_gather(1)
    message_arrive(1)
    forward_pass(1, range(1, 2))
    products(1)
    reduce_side(1)
    reduce_line(1)
    forward_pass(1, range(2, nz))
    reduce_end(1)

    for o in range(1, nd):
        c = copy(tdst.at[me_d], tdst.at[me_d], send_td.at[o - 1], recv_td.at[me_d],
                 at_dst((me_d + o) % nd))
        c.start()
        pending.append(c)
    for o in range(1, nd):
        e = (me_d + o) % nd
        copy(tdst.at[e], tdst.at[e], send_td.at[o - 1], recv_td.at[e], at_dst(e)).wait_recv()
    tsrc[me_s] = sum(tdst[d] for d in range(nd))
    for o in range(1, ns):
        c = copy(tsrc.at[me_s], tsrc.at[me_s], send_ts.at[o - 1], recv_ts.at[me_s],
                 at_src((me_s + o) % ns))
        c.start()
        pending.append(c)
    for o in range(1, ns):
        e = (me_s + o) % ns
        copy(tsrc.at[e], tsrc.at[e], send_ts.at[o - 1], recv_ts.at[e], at_src(e)).wait_recv()
    whole = sum(tsrc[s] for s in range(ns))
    norm = jnp.sum(whole, axis=1, keepdims=True) / total_states
    norm = jnp.broadcast_to(norm, (2 * seqs, blk))
    scales[...] = norm
    inverse = 1.0 / norm

    def finish(a, carry):
        beta[a] = beta[a] / norm[seqs:]
        return carry

    lax.fori_loop(0, local, finish, 0)

    for k in range(2):
        gather_end(fwds, k, me_d, nz, mate_d, send_f, recv_f)

    def count(m, carry):
        r, c = table[3 * slots + m], table[4 * slots + m]
        left = jnp.concatenate([fwds[k][r // local, r % local] for k in range(2)], axis=0)
        right = jnp.concatenate([msgs[k][c // local, c % local] for k in range(2)], axis=0)
        right = (right.astype(jnp.float32) * inverse).astype(jnp.bfloat16)
        value = lax.dot_general(left, right, (((0,), (0,)), ((), ())),
                                preferred_element_type=jnp.float32)
        counts[m] = (value * trans[m].astype(jnp.float32) * table[5 * slots + m].astype(jnp.float32)).astype(jnp.bfloat16)
        return carry

    lax.fori_loop(0, slots, count, 0, unroll=4)
    for c in pending:
        c.wait_send()


def body(nd, ns, transitions, row_block, col_block, beta_last, emissions, forward):
    seqs, local, _, blk = beta_last.shape
    slots = transitions.shape[0]
    columns, rows = local * ns, local * nd
    total_states = rows * ns * blk

    live = row_block >= 0
    row = jnp.where(live, row_block // ns, 0)
    col = jnp.where(live, col_block % columns, 0)
    col = col % ns * local + col // ns
    key = jnp.where(live, row, rows)
    number = jnp.arange(slots)
    before = (key[None, :] < key[:, None]) | (
        (key[None, :] == key[:, None]) & (number[None, :] < number[:, None]))
    rank = jnp.sum(before.astype(jnp.int32), axis=1)
    place = (rank[None, :] == number[:, None]).astype(jnp.int32)
    perm = jnp.sum(place * number[None, :].astype(jnp.int32), axis=1)
    pcol = jnp.sum(place * col[None, :], axis=1)
    same = jnp.any((key[None, :] == key[:, None]) & (rank[None, :] == rank[:, None] - 1), axis=1)
    flag = jnp.sum(place * same[None, :].astype(jnp.int32), axis=1)
    every = jnp.arange(rows)
    last = jnp.where(jnp.any(key[None, :] == every[:, None], axis=1),
                     jnp.sum((key[None, :] <= every[:, None]).astype(jnp.int32), axis=1), 0)

    table = jnp.concatenate(
        [perm, pcol, flag, row, col, live.astype(jnp.int32), last]).astype(jnp.int32)

    def by_block(array):
        return jnp.swapaxes(array[..., 0, :], -3, -2)

    msg0 = by_block((emissions[0].astype(jnp.float32) * beta_last).astype(jnp.bfloat16))
    em1 = by_block(emissions[1])
    fwd = by_block(forward)

    smem = pl.BlockSpec(memory_space=pltpu.SMEM)
    vmem = pl.BlockSpec(memory_space=pltpu.VMEM)
    nz, nx = nd // 2, ns // 2
    block = (local, seqs, blk)
    dma = pltpu.SemaphoreType.DMA
    counts, beta, scales = pl.pallas_call(
        functools.partial(kernel, nd, ns, float(total_states)),
        out_shape=(
            jax.ShapeDtypeStruct(transitions.shape, jnp.bfloat16),
            jax.ShapeDtypeStruct(block, jnp.float32),
            jax.ShapeDtypeStruct((2 * seqs, blk), jnp.float32),
        ),
        in_specs=[smem] + [vmem] * 4,
        out_specs=(vmem, vmem, vmem),
        scratch_shapes=[
            pltpu.VMEM((ns,) + block, jnp.bfloat16),
            pltpu.VMEM((ns,) + block, jnp.bfloat16),
            pltpu.VMEM((nd,) + block, jnp.bfloat16),
            pltpu.VMEM((nd,) + block, jnp.bfloat16),
            pltpu.VMEM((slots + 1, seqs, blk), jnp.float32),
            pltpu.VMEM((2, nd) + block, jnp.bfloat16),
            pltpu.VMEM((2, nz) + block, jnp.bfloat16),
            pltpu.VMEM((2, nz) + block, jnp.bfloat16),
            pltpu.VMEM((2, nz) + block, jnp.bfloat16),
            pltpu.VMEM((nd, 2 * seqs, blk), jnp.float32),
            pltpu.VMEM((ns, 2 * seqs, blk), jnp.float32),
            dma((2, 2 * nx)), dma((2, ns)),
            dma((2, 2 * nz)), dma((2, nd)),
            dma((2, nz)), dma((2, nz)),
            dma((2, nz)), dma((2, nz)),
            dma((nd,)), dma((nd,)),
            dma((ns,)), dma((ns,)),
        ],
        compiler_params=pltpu.CompilerParams(
            collective_id=0, has_side_effects=True, vmem_limit_bytes=48 * 1024 * 1024),
    )(table, transitions, msg0, em1, fwd)
    first, second = scales[:seqs, 0], scales[seqs:, 0]
    logs = jnp.log(jnp.stack([first, second / first]))
    return counts, jnp.swapaxes(beta, 0, 1)[:, :, None, :], logs


def solution(mesh):
    return jax.shard_map(
        functools.partial(body, mesh.shape["dst"], mesh.shape["src"]),
        mesh=mesh,
        in_specs=(
            P(("dst", "src"), None, None),
            P(("dst", "src")),
            P(("dst", "src")),
            P(None, "dst", "src", None),
            P(None, None, "dst", "src", None),
            P(None, None, "dst", "src", None),
        ),
        out_specs=(P(("dst", "src"), None, None), P(None, "dst", "src", None), P()),
        check_vma=False,
    )
```

```python
import functools

import jax
import jax.numpy as jnp
from jax import lax
from jax.experimental import pallas as pl
from jax.experimental.pallas import tpu as pltpu
from jax.sharding import PartitionSpec as P

MESH = pl.DeviceIdType.MESH


def kernel(nd, ns, total_states, table,
           last_in, trans, msg0, em1, fwd, counts, beta, scales,
           msgs0, msgs1, fwds0, fwds1, prods0, prods1, runs0, runs1,
           mates0, mates1, last_mate, last_table, zsend, zpart, tdst, tsrc,
           send_m, recv_m, send_f, recv_f, send_y, recv_y, send_z, recv_z,
           send_td, recv_td, send_ts, recv_ts, send_l, recv_l, local_l):
    local, seqs, blk = msg0.shape
    slots = trans.shape[0]
    nz, nx = nd // 2, ns // 2
    me_d, me_s = lax.axis_index("dst"), lax.axis_index("src")
    z, y = me_d // 2, me_d % 2
    x, core = me_s // 2, me_s % 2

    def at_dst(d):
        return (d, me_s)

    def at_src(s):
        return (me_d, s)

    def copy(src, dst, ssem, rsem, dev):
        return pltpu.make_async_remote_copy(
            src_ref=src, dst_ref=dst, send_sem=ssem, recv_sem=rsem,
            device_id=dev, device_id_type=MESH)

    barrier = pltpu.get_barrier_semaphore()
    for o in range(1, nd):
        pl.semaphore_signal(barrier, inc=1, device_id=at_dst((me_d + o) % nd), device_id_type=MESH)
    for o in range(1, ns):
        pl.semaphore_signal(barrier, inc=1, device_id=at_src((me_s + o) % ns), device_id_type=MESH)
    pl.semaphore_wait(barrier, nd + ns - 2)

    msgs, fwds = (msgs0, msgs1), (fwds0, fwds1)
    prods, runs, mates = (prods0, prods1), (runs0, runs1), (mates0, mates1)
    chunks = send_y.shape[1]
    part = slots // chunks
    pending = []

    def other(pos, o):
        for bit in range(o.bit_length()):
            if o >> bit & 1:
                pos = pos + (1 << bit) - 2 * (pos // (1 << bit) % 2) * (1 << bit)
        return pos

    def gather_side(buf, k, me, side_dev, ssem, rsem):
        c = copy(buf[k].at[me], buf[k].at[me], ssem.at[k, 0], rsem.at[k, me], side_dev)
        c.start()
        pending.append(c)

    def gather_line(buf, k, me, count, dev, ssem, rsem):
        pos, side = me // 2, me % 2
        for o in range(1, count):
            c = copy(buf[k].at[me], buf[k].at[me], ssem.at[k, o], rsem.at[k, me],
                     dev(other(pos, o) * 2 + side))
            c.start()
            pending.append(c)

    def gather_pass(buf, k, me, offsets, count, side_dev, ssem, rsem):
        pos, side = me // 2, me % 2
        for o in offsets:
            e = other(pos, o) * 2 + side
            c = copy(buf[k].at[e], buf[k].at[e], ssem.at[k, count + o - 1], rsem.at[k, e], side_dev)
            c.wait_recv()
            c.start()
            pending.append(c)

    def gather_end(buf, k, me, count, side_dev, ssem, rsem):
        pos, side = me // 2, me % 2
        for o in range(count):
            e = other(pos, o) * 2 + 1 - side
            copy(buf[k].at[e], buf[k].at[e], ssem.at[k, 0], rsem.at[k, e], side_dev).wait_recv()

    mate_d = at_dst(z * 2 + 1 - y)
    mate_s = at_src(x * 2 + 1 - core)

    def message_gather(k):
        gather_line(msgs, k, me_s, nx, at_src, send_m, recv_m)
        gather_side(msgs, k, me_s, mate_s, send_m, recv_m)

    def message_arrive(k):
        gather_pass(msgs, k, me_s, range(1, nx), nx, mate_s, send_m, recv_m)
        gather_end(msgs, k, me_s, nx, mate_s, send_m, recv_m)

    def forward_pass(k, offsets):
        gather_pass(fwds, k, me_d, offsets, nz, mate_d, send_f, recv_f)

    def rows_of(k, chunk):
        piece = pl.ds(1 + chunk * part, part)
        return copy(runs[k].at[piece], mates[k].at[piece], send_y.at[k, chunk],
                    recv_y.at[k, chunk], mate_d)

    def products(k):
        acc = jnp.zeros((seqs, blk), jnp.float32)
        runs[k][0] = acc.astype(jnp.bfloat16)
        mates[k][0] = acc.astype(jnp.bfloat16)
        for chunk in range(chunks):
            def one(j, carry):
                c = table[slots + j]
                prods[k][j] = lax.dot_general(
                    msgs[k][c // local, c % local], trans[table[j]], (((1,), (1,)), ((), ())),
                    preferred_element_type=jnp.float32)
                return carry

            def add_run(j, acc):
                acc = prods[k][j] + acc * table[2 * slots + j].astype(jnp.float32)
                runs[k][j + 1] = acc.astype(jnp.bfloat16)
                return acc

            lax.fori_loop(chunk * part, (chunk + 1) * part, one, 0, unroll=8)
            acc = lax.fori_loop(chunk * part, (chunk + 1) * part, add_run, acc, unroll=4)
            c = rows_of(k, chunk)
            c.start()
            pending.append(c)

    def two_rows(k, d, a):
        r = d * local + a
        own = runs[k][table[8 * slots + r]]
        mate = mates[k][last_table[r // 128, r % 128]]
        return own.astype(jnp.float32) + mate.astype(jnp.float32)

    def reduce_line(k):
        for chunk in range(chunks):
            rows_of(k, chunk).wait_recv()
        for o in reversed(range(1, nz)):
            zt = other(z, o)

            def add(a, carry):
                zsend[k, zt, a] = two_rows(k, zt * 2 + y, a).astype(jnp.bfloat16)
                return carry

            lax.fori_loop(0, local, add, 0, unroll=4)
            c = copy(zsend.at[k, zt], zpart.at[k, z], send_z.at[k, o - 1], recv_z.at[k, z],
                     at_dst(zt * 2 + y))
            c.start()
            pending.append(c)

    def reduce_end(k, use):
        for o in range(1, nz):
            zf = other(z, o)
            copy(zsend.at[k, zf], zpart.at[k, zf], send_z.at[k, o - 1], recv_z.at[k, zf],
                 mate_d).wait_recv()

        def add(a, carry):
            raw = two_rows(k, me_d, a)
            for o in range(1, nz):
                raw = raw + zpart[k, other(z, o), a].astype(jnp.float32)
            use(a, raw)
            return carry

        lax.fori_loop(0, local, add, 0, unroll=2)

    def terms(k):
        def term(j, total):
            r = table[6 * slots + j]
            value = prods[k][j] * fwds[k][r // local, r % local].astype(jnp.float32)
            return total + value * table[7 * slots + j].astype(jnp.float32)

        tdst[me_d, pl.ds(k * seqs, seqs)] = lax.fori_loop(
            0, slots, term, jnp.zeros((seqs, blk), jnp.float32), unroll=4)

    def keep_message(a, carry):
        msgs[0][me_s, a] = msg0[a]
        return carry

    lax.fori_loop(0, local, keep_message, 0, unroll=4)
    message_gather(0)
    last_copy = copy(last_in, last_mate, send_l, recv_l, mate_d)
    last_copy.start()
    pending.append(last_copy)
    for k in range(2):
        def keep_forward(a, carry, k=k):
            fwds[k][me_d, a] = fwd[k, a]
            return carry

        lax.fori_loop(0, local, keep_forward, 0, unroll=4)
    gather_line(fwds, 0, me_d, nz, at_dst, send_f, recv_f)
    gather_side(fwds, 0, me_d, mate_d, send_f, recv_f)
    last_copy.wait_recv()
    to_table = pltpu.make_async_copy(last_mate, last_table, local_l)
    to_table.start()
    to_table.wait()
    message_arrive(0)
    forward_pass(0, range(1, 2))
    products(0)
    reduce_line(0)
    forward_pass(0, range(2, nz))
    gather_side(fwds, 1, me_d, mate_d, send_f, recv_f)

    def next_message(a, raw):
        msgs[1][me_s, a] = (em1[a].astype(jnp.float32) * raw).astype(jnp.bfloat16)

    reduce_end(0, next_message)

    message_gather(1)
    gather_line(fwds, 1, me_d, nz, at_dst, send_f, recv_f)
    message_arrive(1)
    forward_pass(1, range(1, 2))
    products(1)
    reduce_line(1)
    forward_pass(1, range(2, nz))
    for k in range(2):
        gather_end(fwds, k, me_d, nz, mate_d, send_f, recv_f)
        terms(k)

    for o in range(1, nd):
        c = copy(tdst.at[me_d], tdst.at[me_d], send_td.at[o - 1], recv_td.at[me_d],
                 at_dst((me_d + o) % nd))
        c.start()
        pending.append(c)
    for o in range(1, nd):
        e = (me_d + o) % nd
        copy(tdst.at[e], tdst.at[e], send_td.at[o - 1], recv_td.at[e], at_dst(e)).wait_recv()
    tsrc[me_s] = sum(tdst[d] for d in range(nd))
    for o in range(1, ns):
        c = copy(tsrc.at[me_s], tsrc.at[me_s], send_ts.at[o - 1], recv_ts.at[me_s],
                 at_src((me_s + o) % ns))
        c.start()
        pending.append(c)
    for o in range(1, ns):
        e = (me_s + o) % ns
        copy(tsrc.at[e], tsrc.at[e], send_ts.at[o - 1], recv_ts.at[e], at_src(e)).wait_recv()
    whole = sum(tsrc[s] for s in range(ns))
    norm = jnp.sum(whole, axis=1, keepdims=True) / total_states
    norm = jnp.broadcast_to(norm, (2 * seqs, blk))
    scales[...] = norm
    inverse = 1.0 / norm

    def count(m, carry):
        r, c = table[3 * slots + m], table[4 * slots + m]
        left = jnp.concatenate([fwds[k][r // local, r % local] for k in range(2)], axis=0)
        right = jnp.concatenate([msgs[k][c // local, c % local] for k in range(2)], axis=0)
        right = (right.astype(jnp.float32) * inverse).astype(jnp.bfloat16)
        value = lax.dot_general(left, right, (((0,), (0,)), ((), ())),
                                preferred_element_type=jnp.float32)
        counts[m] = (value * trans[m].astype(jnp.float32) * table[5 * slots + m].astype(jnp.float32)).astype(jnp.bfloat16)
        return carry

    lax.fori_loop(0, slots, count, 0, unroll=4)

    def last_beta(a, raw):
        beta[a] = raw * inverse[seqs:]

    reduce_end(1, last_beta)
    for c in pending:
        c.wait_send()


def body(nd, ns, transitions, row_block, col_block, beta_last, emissions, forward):
    seqs, local, _, blk = beta_last.shape
    slots = transitions.shape[0]
    columns, rows = local * ns, local * nd
    total_states = rows * ns * blk

    live = row_block >= 0
    row = jnp.where(live, row_block // ns, 0)
    col = jnp.where(live, col_block % columns, 0)
    col = col % ns * local + col // ns
    key = jnp.where(live, row, rows)
    number = jnp.arange(slots)
    before = (key[None, :] < key[:, None]) | (
        (key[None, :] == key[:, None]) & (number[None, :] < number[:, None]))
    rank = jnp.sum(before.astype(jnp.int32), axis=1)
    place = (rank[None, :] == number[:, None]).astype(jnp.int32)
    perm = jnp.sum(place * number[None, :].astype(jnp.int32), axis=1)
    pcol = jnp.sum(place * col[None, :], axis=1)
    same = jnp.any((key[None, :] == key[:, None]) & (rank[None, :] == rank[:, None] - 1), axis=1)
    flag = jnp.sum(place * same[None, :].astype(jnp.int32), axis=1)
    every = jnp.arange(rows)
    prow = jnp.sum(place * row[None, :], axis=1)
    plive = jnp.sum(place * live[None, :].astype(jnp.int32), axis=1)
    last = jnp.where(jnp.any(key[None, :] == every[:, None], axis=1),
                     jnp.sum((key[None, :] <= every[:, None]).astype(jnp.int32), axis=1), 0)

    table = jnp.concatenate(
        [perm, pcol, flag, row, col, live.astype(jnp.int32), prow, plive, last]).astype(jnp.int32)

    lines = -(-rows // 128)
    last2 = jnp.pad(last.astype(jnp.int32), (0, lines * 128 - rows)).reshape(lines, 128)

    def by_block(array):
        return jnp.swapaxes(array[..., 0, :], -3, -2)

    msg0 = by_block((emissions[0].astype(jnp.float32) * beta_last).astype(jnp.bfloat16))
    em1 = by_block(emissions[1])
    fwd = by_block(forward)

    smem = pl.BlockSpec(memory_space=pltpu.SMEM)
    vmem = pl.BlockSpec(memory_space=pltpu.VMEM)
    nz, nx = nd // 2, ns // 2
    block = (local, seqs, blk)
    dma = pltpu.SemaphoreType.DMA
    counts, beta, scales = pl.pallas_call(
        functools.partial(kernel, nd, ns, float(total_states)),
        out_shape=(
            jax.ShapeDtypeStruct(transitions.shape, jnp.bfloat16),
            jax.ShapeDtypeStruct(block, jnp.float32),
            jax.ShapeDtypeStruct((2 * seqs, blk), jnp.float32),
        ),
        in_specs=[smem] + [vmem] * 5,
        out_specs=(vmem, vmem, vmem),
        scratch_shapes=[
            pltpu.VMEM((ns,) + block, jnp.bfloat16),
            pltpu.VMEM((ns,) + block, jnp.bfloat16),
            pltpu.VMEM((nd,) + block, jnp.bfloat16),
            pltpu.VMEM((nd,) + block, jnp.bfloat16),
            pltpu.VMEM((slots, seqs, blk), jnp.float32),
            pltpu.VMEM((slots, seqs, blk), jnp.float32),
            pltpu.VMEM((slots + 1, seqs, blk), jnp.bfloat16),
            pltpu.VMEM((slots + 1, seqs, blk), jnp.bfloat16),
            pltpu.VMEM((slots + 1, seqs, blk), jnp.bfloat16),
            pltpu.VMEM((slots + 1, seqs, blk), jnp.bfloat16),
            pltpu.VMEM((lines, 128), jnp.int32),
            pltpu.SMEM((lines, 128), jnp.int32),
            pltpu.VMEM((2, nz) + block, jnp.bfloat16),
            pltpu.VMEM((2, nz) + block, jnp.bfloat16),
            pltpu.VMEM((nd, 2 * seqs, blk), jnp.float32),
            pltpu.VMEM((ns, 2 * seqs, blk), jnp.float32),
            dma((2, 2 * nx)), dma((2, ns)),
            dma((2, 2 * nz)), dma((2, nd)),
            dma((2, 4)), dma((2, 4)),
            dma((2, nz)), dma((2, nz)),
            dma((nd,)), dma((nd,)),
            dma((ns,)), dma((ns,)),
            dma, dma, dma,
        ],
        compiler_params=pltpu.CompilerParams(
            collective_id=0, has_side_effects=True, vmem_limit_bytes=48 * 1024 * 1024),
    )(table, last2, transitions, msg0, em1, fwd)
    first, second = scales[:seqs, 0], scales[seqs:, 0]
    logs = jnp.log(jnp.stack([first, second / first]))
    return counts, jnp.swapaxes(beta, 0, 1)[:, :, None, :], logs


def solution(mesh):
    return jax.shard_map(
        functools.partial(body, mesh.shape["dst"], mesh.shape["src"]),
        mesh=mesh,
        in_specs=(
            P(("dst", "src"), None, None),
            P(("dst", "src")),
            P(("dst", "src")),
            P(None, "dst", "src", None),
            P(None, None, "dst", "src", None),
            P(None, None, "dst", "src", None),
        ),
        out_specs=(P(("dst", "src"), None, None), P(None, "dst", "src", None), P()),
        check_vma=False,
    )
```

```python
import functools

import jax
import jax.numpy as jnp
from jax import lax
from jax.experimental import pallas as pl
from jax.experimental.pallas import tpu as pltpu
from jax.sharding import PartitionSpec as P

MESH = pl.DeviceIdType.MESH


def kernel(nd, ns, total_states, table,
           last_in, trans, msg0, em1, fwd, counts, beta, scales,
           msgs0, msgs1, fwds0, fwds1, prods0, prods1, runs0, runs1,
           mates0, mates1, last_mate, last_table, zsend, zpart, tdst, tsrc,
           send_m, recv_m, send_f, recv_f, send_y, recv_y, send_z, recv_z,
           send_td, recv_td, send_ts, recv_ts, send_l, recv_l, local_l, send_p, send_r):
    local, seqs, blk = msg0.shape
    slots = trans.shape[0]
    nz, nx = nd // 2, ns // 2
    me_d, me_s = lax.axis_index("dst"), lax.axis_index("src")
    z, y = me_d // 2, me_d % 2
    x, core = me_s // 2, me_s % 2

    def at_dst(d):
        return (d, me_s)

    def at_src(s):
        return (me_d, s)

    def copy(src, dst, ssem, rsem, dev):
        return pltpu.make_async_remote_copy(
            src_ref=src, dst_ref=dst, send_sem=ssem, recv_sem=rsem,
            device_id=dev, device_id_type=MESH)

    barrier = pltpu.get_barrier_semaphore()
    for o in range(1, nd):
        pl.semaphore_signal(barrier, inc=1, device_id=at_dst((me_d + o) % nd), device_id_type=MESH)
    for o in range(1, ns):
        pl.semaphore_signal(barrier, inc=1, device_id=at_src((me_s + o) % ns), device_id_type=MESH)
    pl.semaphore_wait(barrier, nd + ns - 2)

    msgs, fwds = (msgs0, msgs1), (fwds0, fwds1)
    prods, runs, mates = (prods0, prods1), (runs0, runs1), (mates0, mates1)
    chunks = send_y.shape[1]
    part = slots // chunks
    pending, guards = [], []
    first_way = 1 - z // (nz // 2)

    def other(pos, o):
        for bit in range(o.bit_length()):
            if o >> bit & 1:
                pos = pos + (1 << bit) - 2 * (pos // (1 << bit) % 2) * (1 << bit)
        return pos

    def gather_side(buf, k, me, side_dev, ssem, rsem):
        c = copy(buf[k].at[me], buf[k].at[me], ssem.at[k, 0], rsem.at[k, me], side_dev)
        c.start()
        pending.append(c)

    def gather_line(buf, k, me, count, dev, ssem, rsem):
        pos, side = me // 2, me % 2
        for o in range(1, count):
            c = copy(buf[k].at[me], buf[k].at[me], ssem.at[k, o], rsem.at[k, me],
                     dev(other(pos, o) * 2 + side))
            c.start()
            pending.append(c)

    def gather_pass(buf, k, me, offsets, count, side_dev, ssem, rsem):
        pos, side = me // 2, me % 2
        for o in offsets:
            e = other(pos, o) * 2 + side
            c = copy(buf[k].at[e], buf[k].at[e], ssem.at[k, count + o - 1], rsem.at[k, e], side_dev)
            c.wait_recv()
            c.start()
            pending.append(c)

    def gather_end(buf, k, me, count, side_dev, ssem, rsem):
        pos, side = me // 2, me % 2
        for o in range(count):
            e = other(pos, o) * 2 + 1 - side
            copy(buf[k].at[e], buf[k].at[e], ssem.at[k, 0], rsem.at[k, e], side_dev).wait_recv()

    mate_d = at_dst(z * 2 + 1 - y)
    mate_s = at_src(x * 2 + 1 - core)

    def message_gather(k):
        gather_line(msgs, k, me_s, nx, at_src, send_m, recv_m)
        gather_side(msgs, k, me_s, mate_s, send_m, recv_m)

    def message_arrive(k):
        gather_pass(msgs, k, me_s, range(1, nx), nx, mate_s, send_m, recv_m)
        gather_end(msgs, k, me_s, nx, mate_s, send_m, recv_m)

    def guarded(cond, make):
        pl.when(cond)(lambda: make().start())
        guards.append((cond, make))

    def forward_line(k):
        def to(step):
            return lambda: copy(fwds[k].at[me_d], fwds[k].at[me_d], send_f.at[k, 1 + step],
                                recv_f.at[k, me_d], at_dst((z - 1 + 2 * step) * 2 + y))

        guarded(z < nz - 1, to(1))
        guarded(z > 0, to(0))

    def forward_hop(k, h):
        for sign, there, more in ((-1, z >= h, z < nz - 1), (1, z + h <= nz - 1, z > 0)):
            e = (z + sign * h) * 2 + y
            block = fwds[k].at[e]

            def relay(e=e, block=block, sign=sign):
                return copy(block, block, send_r.at[k, e], recv_f.at[k, e],
                            at_dst((z - sign) * 2 + y))

            def across(e=e, block=block):
                return copy(block, block, send_p.at[k, e], recv_f.at[k, e], mate_d)

            pl.when(there)(lambda across=across: across().wait_recv())
            guarded(there & more, relay)
            guarded(there, across)

    def rows_of(k, chunk):
        piece = pl.ds(1 + chunk * part, part)
        return copy(runs[k].at[piece], mates[k].at[piece], send_y.at[k, chunk],
                    recv_y.at[k, chunk], mate_d)

    def products(k):
        acc = jnp.zeros((seqs, blk), jnp.float32)
        runs[k][0] = acc.astype(jnp.bfloat16)
        mates[k][0] = acc.astype(jnp.bfloat16)
        for chunk in range(chunks):
            def one(j, carry):
                c = table[slots + j]
                prods[k][j] = lax.dot_general(
                    msgs[k][c // local, c % local], trans[table[j]], (((1,), (1,)), ((), ())),
                    preferred_element_type=jnp.float32)
                return carry

            def add_run(j, acc):
                acc = prods[k][j] + acc * table[2 * slots + j].astype(jnp.float32)
                runs[k][j + 1] = acc.astype(jnp.bfloat16)
                return acc

            lax.fori_loop(chunk * part, (chunk + 1) * part, one, 0, unroll=8)
            acc = lax.fori_loop(chunk * part, (chunk + 1) * part, add_run, acc, unroll=4)
            c = rows_of(k, chunk)
            c.start()
            pending.append(c)

    def two_rows(k, d, a):
        r = d * local + a
        own = runs[k][table[8 * slots + r]]
        mate = mates[k][last_table[r // 128, r % 128]]
        return own.astype(jnp.float32) + mate.astype(jnp.float32)

    def reduce_line(k):
        for chunk in range(chunks):
            rows_of(k, chunk).wait_recv()
        for turn in range(2):
            way = first_way if turn == 0 else 1 - first_way
            step = 2 * way - 1
            count = way * (nz - 1 - z) + (1 - way) * z
            before = z * way + (nz - 1 - z) * (1 - way)
            for q in reversed(range(1, nz)):
                zt = z + step * q

                def send(zt=zt, way=way, step=step):
                    return copy(zsend.at[k, zt], zpart.at[k, way, zt], send_z.at[k, zt],
                                recv_z.at[k, way, zt], at_dst((z + step) * 2 + y))

                def work(zt=zt, way=way, send=send):
                    def add(a, carry):
                        zsend[k, zt, a] = (two_rows(k, zt * 2 + y, a)
                                           + zpart[k, way, zt, a].astype(jnp.float32)
                                           ).astype(jnp.bfloat16)
                        return carry

                    lax.fori_loop(0, local, add, 0, unroll=4)
                    send().start()

                pl.when((q <= count) & (before > 0))(lambda send=send: send().wait_recv())
                pl.when(q <= count)(work)
                guards.append((q <= count, send))

    def reduce_end(k, use):
        def arrived(way):
            return lambda: copy(zsend.at[k, z], zpart.at[k, way, z], send_z.at[k, z],
                                recv_z.at[k, way, z], mate_d).wait_recv()

        pl.when(z > 0)(arrived(1))
        pl.when(z < nz - 1)(arrived(0))

        def add(a, carry):
            raw = (two_rows(k, me_d, a) + zpart[k, 0, z, a].astype(jnp.float32)
                   + zpart[k, 1, z, a].astype(jnp.float32))
            use(a, raw)
            return carry

        lax.fori_loop(0, local, add, 0, unroll=2)

    def clear(way):
        def run():
            def one(a, carry):
                for k in range(2):
                    for zt in range(nz):
                        zpart[k, way, zt, a] = jnp.zeros((seqs, blk), jnp.bfloat16)
                return carry

            lax.fori_loop(0, local, one, 0)
        return run

    def terms(k):
        def term(j, total):
            r = table[6 * slots + j]
            value = prods[k][j] * fwds[k][r // local, r % local].astype(jnp.float32)
            return total + value * table[7 * slots + j].astype(jnp.float32)

        tdst[me_d, pl.ds(k * seqs, seqs)] = lax.fori_loop(
            0, slots, term, jnp.zeros((seqs, blk), jnp.float32), unroll=4)

    def keep_message(a, carry):
        msgs[0][me_s, a] = msg0[a]
        return carry

    lax.fori_loop(0, local, keep_message, 0, unroll=4)
    message_gather(0)
    last_copy = copy(last_in, last_mate, send_l, recv_l, mate_d)
    last_copy.start()
    pending.append(last_copy)
    for k in range(2):
        def keep_forward(a, carry, k=k):
            fwds[k][me_d, a] = fwd[k, a]
            return carry

        lax.fori_loop(0, local, keep_forward, 0, unroll=4)
    forward_line(0)
    gather_side(fwds, 0, me_d, mate_d, send_f, recv_f)
    last_copy.wait_recv()
    to_table = pltpu.make_async_copy(last_mate, last_table, local_l)
    to_table.start()
    to_table.wait()
    pl.when(z == 0)(clear(1))
    pl.when(z == nz - 1)(clear(0))
    message_arrive(0)
    forward_hop(0, 1)
    products(0)
    reduce_line(0)
    for h in range(2, nz):
        forward_hop(0, h)
    gather_side(fwds, 1, me_d, mate_d, send_f, recv_f)

    def next_message(a, raw):
        msgs[1][me_s, a] = (em1[a].astype(jnp.float32) * raw).astype(jnp.bfloat16)

    reduce_end(0, next_message)

    message_gather(1)
    forward_line(1)
    message_arrive(1)
    forward_hop(1, 1)
    products(1)
    reduce_line(1)
    for h in range(2, nz):
        forward_hop(1, h)
    for k in range(2):
        gather_end(fwds, k, me_d, nz, mate_d, send_f, recv_f)
        terms(k)

    for o in range(1, nd):
        c = copy(tdst.at[me_d], tdst.at[me_d], send_td.at[o - 1], recv_td.at[me_d],
                 at_dst((me_d + o) % nd))
        c.start()
        pending.append(c)
    for o in range(1, nd):
        e = (me_d + o) % nd
        copy(tdst.at[e], tdst.at[e], send_td.at[o - 1], recv_td.at[e], at_dst(e)).wait_recv()
    tsrc[me_s] = sum(tdst[d] for d in range(nd))
    for o in range(1, ns):
        c = copy(tsrc.at[me_s], tsrc.at[me_s], send_ts.at[o - 1], recv_ts.at[me_s],
                 at_src((me_s + o) % ns))
        c.start()
        pending.append(c)
    for o in range(1, ns):
        e = (me_s + o) % ns
        copy(tsrc.at[e], tsrc.at[e], send_ts.at[o - 1], recv_ts.at[e], at_src(e)).wait_recv()
    whole = sum(tsrc[s] for s in range(ns))
    norm = jnp.sum(whole, axis=1, keepdims=True) / total_states
    norm = jnp.broadcast_to(norm, (2 * seqs, blk))
    scales[...] = norm
    inverse = 1.0 / norm

    def count(m, carry):
        r, c = table[3 * slots + m], table[4 * slots + m]
        left = jnp.concatenate([fwds[k][r // local, r % local] for k in range(2)], axis=0)
        right = jnp.concatenate([msgs[k][c // local, c % local] for k in range(2)], axis=0)
        right = (right.astype(jnp.float32) * inverse).astype(jnp.bfloat16)
        value = lax.dot_general(left, right, (((0,), (0,)), ((), ())),
                                preferred_element_type=jnp.float32)
        counts[m] = (value * trans[m].astype(jnp.float32) * table[5 * slots + m].astype(jnp.float32)).astype(jnp.bfloat16)
        return carry

    lax.fori_loop(0, slots, count, 0, unroll=4)

    def last_beta(a, raw):
        beta[a] = raw * inverse[seqs:]

    reduce_end(1, last_beta)
    for c in pending:
        c.wait_send()
    for cond, make in guards:
        pl.when(cond)(lambda make=make: make().wait_send())


def body(nd, ns, transitions, row_block, col_block, beta_last, emissions, forward):
    seqs, local, _, blk = beta_last.shape
    slots = transitions.shape[0]
    columns, rows = local * ns, local * nd
    total_states = rows * ns * blk

    live = row_block >= 0
    row = jnp.where(live, row_block // ns, 0)
    col = jnp.where(live, col_block % columns, 0)
    col = col % ns * local + col // ns
    key = jnp.where(live, row, rows)
    number = jnp.arange(slots)
    before = (key[None, :] < key[:, None]) | (
        (key[None, :] == key[:, None]) & (number[None, :] < number[:, None]))
    rank = jnp.sum(before.astype(jnp.int32), axis=1)
    place = (rank[None, :] == number[:, None]).astype(jnp.int32)
    perm = jnp.sum(place * number[None, :].astype(jnp.int32), axis=1)
    pcol = jnp.sum(place * col[None, :], axis=1)
    same = jnp.any((key[None, :] == key[:, None]) & (rank[None, :] == rank[:, None] - 1), axis=1)
    flag = jnp.sum(place * same[None, :].astype(jnp.int32), axis=1)
    every = jnp.arange(rows)
    prow = jnp.sum(place * row[None, :], axis=1)
    plive = jnp.sum(place * live[None, :].astype(jnp.int32), axis=1)
    last = jnp.where(jnp.any(key[None, :] == every[:, None], axis=1),
                     jnp.sum((key[None, :] <= every[:, None]).astype(jnp.int32), axis=1), 0)

    table = jnp.concatenate(
        [perm, pcol, flag, row, col, live.astype(jnp.int32), prow, plive, last]).astype(jnp.int32)

    lines = -(-rows // 128)
    last2 = jnp.pad(last.astype(jnp.int32), (0, lines * 128 - rows)).reshape(lines, 128)

    def by_block(array):
        return jnp.swapaxes(array[..., 0, :], -3, -2)

    msg0 = by_block((emissions[0].astype(jnp.float32) * beta_last).astype(jnp.bfloat16))
    em1 = by_block(emissions[1])
    fwd = by_block(forward)

    smem = pl.BlockSpec(memory_space=pltpu.SMEM)
    vmem = pl.BlockSpec(memory_space=pltpu.VMEM)
    nz, nx = nd // 2, ns // 2
    block = (local, seqs, blk)
    dma = pltpu.SemaphoreType.DMA
    counts, beta, scales = pl.pallas_call(
        functools.partial(kernel, nd, ns, float(total_states)),
        out_shape=(
            jax.ShapeDtypeStruct(transitions.shape, jnp.bfloat16),
            jax.ShapeDtypeStruct(block, jnp.float32),
            jax.ShapeDtypeStruct((2 * seqs, blk), jnp.float32),
        ),
        in_specs=[smem] + [vmem] * 5,
        out_specs=(vmem, vmem, vmem),
        scratch_shapes=[
            pltpu.VMEM((ns,) + block, jnp.bfloat16),
            pltpu.VMEM((ns,) + block, jnp.bfloat16),
            pltpu.VMEM((nd,) + block, jnp.bfloat16),
            pltpu.VMEM((nd,) + block, jnp.bfloat16),
            pltpu.VMEM((slots, seqs, blk), jnp.float32),
            pltpu.VMEM((slots, seqs, blk), jnp.float32),
            pltpu.VMEM((slots + 1, seqs, blk), jnp.bfloat16),
            pltpu.VMEM((slots + 1, seqs, blk), jnp.bfloat16),
            pltpu.VMEM((slots + 1, seqs, blk), jnp.bfloat16),
            pltpu.VMEM((slots + 1, seqs, blk), jnp.bfloat16),
            pltpu.VMEM((lines, 128), jnp.int32),
            pltpu.SMEM((lines, 128), jnp.int32),
            pltpu.VMEM((2, nz) + block, jnp.bfloat16),
            pltpu.VMEM((2, 2, nz) + block, jnp.bfloat16),
            pltpu.VMEM((nd, 2 * seqs, blk), jnp.float32),
            pltpu.VMEM((ns, 2 * seqs, blk), jnp.float32),
            dma((2, 2 * nx)), dma((2, ns)),
            dma((2, 3)), dma((2, nd)),
            dma((2, 4)), dma((2, 4)),
            dma((2, nz)), dma((2, 2, nz)),
            dma((nd,)), dma((nd,)),
            dma((ns,)), dma((ns,)),
            dma, dma, dma, dma((2, nd)), dma((2, nd)),
        ],
        compiler_params=pltpu.CompilerParams(
            collective_id=0, has_side_effects=True, vmem_limit_bytes=48 * 1024 * 1024),
    )(table, last2, transitions, msg0, em1, fwd)
    first, second = scales[:seqs, 0], scales[seqs:, 0]
    logs = jnp.log(jnp.stack([first, second / first]))
    return counts, jnp.swapaxes(beta, 0, 1)[:, :, None, :], logs


def solution(mesh):
    return jax.shard_map(
        functools.partial(body, mesh.shape["dst"], mesh.shape["src"]),
        mesh=mesh,
        in_specs=(
            P(("dst", "src"), None, None),
            P(("dst", "src")),
            P(("dst", "src")),
            P(None, "dst", "src", None),
            P(None, None, "dst", "src", None),
            P(None, None, "dst", "src", None),
        ),
        out_specs=(P(("dst", "src"), None, None), P(None, "dst", "src", None), P()),
        check_vma=False,
    )
```

```python
import functools

import jax
import jax.numpy as jnp
from jax import lax
from jax.experimental import pallas as pl
from jax.experimental.pallas import tpu as pltpu
from jax.sharding import PartitionSpec as P

MESH = pl.DeviceIdType.MESH


def kernel(nd, ns, total_states, table,
           last_in, trans, msg0, em1, fwd, counts, beta, scales,
           msgs0, msgs1, fwds0, fwds1, prods0, prods1, runs0, runs1,
           mates0, mates1, last_mate, last_table, zsend, zpart, tdst, tsrc,
           send_m, recv_m, send_f, recv_f, send_y, recv_y, send_z, recv_z,
           send_td, recv_td, send_ts, recv_ts, send_l, recv_l, local_l):
    local, seqs, blk = msg0.shape
    slots = trans.shape[0]
    nz, nx = nd // 2, ns // 2
    me_d, me_s = lax.axis_index("dst"), lax.axis_index("src")
    z, y = me_d // 2, me_d % 2
    x, core = me_s // 2, me_s % 2

    def at_dst(d):
        return (d, me_s)

    def at_src(s):
        return (me_d, s)

    def copy(src, dst, ssem, rsem, dev):
        return pltpu.make_async_remote_copy(
            src_ref=src, dst_ref=dst, send_sem=ssem, recv_sem=rsem,
            device_id=dev, device_id_type=MESH)

    barrier = pltpu.get_barrier_semaphore()
    for o in range(1, nd):
        pl.semaphore_signal(barrier, inc=1, device_id=at_dst((me_d + o) % nd), device_id_type=MESH)
    for o in range(1, ns):
        pl.semaphore_signal(barrier, inc=1, device_id=at_src((me_s + o) % ns), device_id_type=MESH)
    pl.semaphore_wait(barrier, nd + ns - 2)

    msgs, fwds = (msgs0, msgs1), (fwds0, fwds1)
    prods, runs, mates = (prods0, prods1), (runs0, runs1), (mates0, mates1)
    chunks = send_y.shape[1]
    part = slots // chunks
    pending = []

    def other(pos, o):
        for bit in range(o.bit_length()):
            if o >> bit & 1:
                pos = pos + (1 << bit) - 2 * (pos // (1 << bit) % 2) * (1 << bit)
        return pos

    def gather_side(buf, k, me, side_dev, ssem, rsem):
        c = copy(buf[k].at[me], buf[k].at[me], ssem.at[k, 0], rsem.at[k, me], side_dev)
        c.start()
        pending.append(c)

    def gather_line(buf, k, me, offsets, dev, ssem, rsem):
        pos, side = me // 2, me % 2
        for o in offsets:
            c = copy(buf[k].at[me], buf[k].at[me], ssem.at[k, o], rsem.at[k, me],
                     dev(other(pos, o) * 2 + side))
            c.start()
            pending.append(c)

    def gather_pass(buf, k, me, offsets, count, side_dev, ssem, rsem):
        pos, side = me // 2, me % 2
        for o in offsets:
            e = other(pos, o) * 2 + side
            c = copy(buf[k].at[e], buf[k].at[e], ssem.at[k, count + o - 1], rsem.at[k, e], side_dev)
            c.wait_recv()
            c.start()
            pending.append(c)

    def gather_end(buf, k, me, count, side_dev, ssem, rsem):
        pos, side = me // 2, me % 2
        for o in range(count):
            e = other(pos, o) * 2 + 1 - side
            copy(buf[k].at[e], buf[k].at[e], ssem.at[k, 0], rsem.at[k, e], side_dev).wait_recv()

    mate_d = at_dst(z * 2 + 1 - y)
    mate_s = at_src(x * 2 + 1 - core)

    def message_gather(k):
        gather_line(msgs, k, me_s, range(1, nx), at_src, send_m, recv_m)
        gather_side(msgs, k, me_s, mate_s, send_m, recv_m)

    def message_arrive(k):
        gather_pass(msgs, k, me_s, range(1, nx), nx, mate_s, send_m, recv_m)
        gather_end(msgs, k, me_s, nx, mate_s, send_m, recv_m)

    def forward_line(k, offsets):
        gather_line(fwds, k, me_d, offsets, at_dst, send_f, recv_f)

    def forward_pass(k, offsets):
        gather_pass(fwds, k, me_d, offsets, nz, mate_d, send_f, recv_f)

    def rows_of(k, chunk):
        piece = pl.ds(1 + chunk * part, part)
        return copy(runs[k].at[piece], mates[k].at[piece], send_y.at[k, chunk],
                    recv_y.at[k, chunk], mate_d)

    def products(k):
        acc = jnp.zeros((seqs, blk), jnp.float32)
        runs[k][0] = acc.astype(jnp.bfloat16)
        mates[k][0] = acc.astype(jnp.bfloat16)
        for chunk in range(chunks):
            def one(j, carry):
                c = table[slots + j]
                prods[k][j] = lax.dot_general(
                    msgs[k][c // local, c % local], trans[table[j]], (((1,), (1,)), ((), ())),
                    preferred_element_type=jnp.float32)
                return carry

            def add_run(j, acc):
                acc = prods[k][j] + acc * table[2 * slots + j].astype(jnp.float32)
                runs[k][j + 1] = acc.astype(jnp.bfloat16)
                return acc

            lax.fori_loop(chunk * part, (chunk + 1) * part, one, 0, unroll=8)
            acc = lax.fori_loop(chunk * part, (chunk + 1) * part, add_run, acc, unroll=4)
            c = rows_of(k, chunk)
            c.start()
            pending.append(c)

    def two_rows(k, d, a):
        r = d * local + a
        own = runs[k][table[8 * slots + r]]
        mate = mates[k][last_table[r // 128, r % 128]]
        return own.astype(jnp.float32) + mate.astype(jnp.float32)

    def reduce_line(k):
        for chunk in range(chunks):
            rows_of(k, chunk).wait_recv()
        for o in reversed(range(1, nz)):
            zt = other(z, o)

            def add(a, carry):
                zsend[k, zt, a] = two_rows(k, zt * 2 + y, a).astype(jnp.bfloat16)
                return carry

            lax.fori_loop(0, local, add, 0, unroll=4)
            c = copy(zsend.at[k, zt], zpart.at[k, z], send_z.at[k, o - 1], recv_z.at[k, z],
                     at_dst(zt * 2 + y))
            c.start()
            pending.append(c)

    def reduce_end(k, use):
        for o in range(1, nz):
            zf = other(z, o)
            copy(zsend.at[k, zf], zpart.at[k, zf], send_z.at[k, o - 1], recv_z.at[k, zf],
                 mate_d).wait_recv()

        def add(a, carry):
            raw = two_rows(k, me_d, a)
            for o in range(1, nz):
                raw = raw + zpart[k, other(z, o), a].astype(jnp.float32)
            use(a, raw)
            return carry

        lax.fori_loop(0, local, add, 0, unroll=2)

    def terms(k):
        def term(j, total):
            r = table[6 * slots + j]
            value = prods[k][j] * fwds[k][r // local, r % local].astype(jnp.float32)
            return total + value * table[7 * slots + j].astype(jnp.float32)

        tdst[me_d, pl.ds(k * seqs, seqs)] = lax.fori_loop(
            0, slots, term, jnp.zeros((seqs, blk), jnp.float32), unroll=4)

    def keep_message(a, carry):
        msgs[0][me_s, a] = msg0[a]
        return carry

    lax.fori_loop(0, local, keep_message, 0, unroll=4)
    message_gather(0)
    last_copy = copy(last_in, last_mate, send_l, recv_l, mate_d)
    last_copy.start()
    pending.append(last_copy)
    for k in range(2):
        def keep_forward(a, carry, k=k):
            fwds[k][me_d, a] = fwd[k, a]
            return carry

        lax.fori_loop(0, local, keep_forward, 0, unroll=4)
    forward_line(0, range(1, 2))
    gather_side(fwds, 0, me_d, mate_d, send_f, recv_f)
    last_copy.wait_recv()
    to_table = pltpu.make_async_copy(last_mate, last_table, local_l)
    to_table.start()
    to_table.wait()
    message_arrive(0)
    forward_line(0, range(2, nz))
    forward_pass(0, range(1, 2))
    products(0)
    reduce_line(0)
    forward_line(1, range(1, 2))
    forward_pass(0, range(2, nz))
    gather_side(fwds, 1, me_d, mate_d, send_f, recv_f)

    def next_message(a, raw):
        msgs[1][me_s, a] = (em1[a].astype(jnp.float32) * raw).astype(jnp.bfloat16)

    reduce_end(0, next_message)

    message_gather(1)
    forward_line(1, range(2, nz))
    message_arrive(1)
    forward_pass(1, range(1, 2))
    products(1)
    reduce_line(1)
    forward_pass(1, range(2, nz))
    for k in range(2):
        gather_end(fwds, k, me_d, nz, mate_d, send_f, recv_f)
        terms(k)

    for o in range(1, nd):
        c = copy(tdst.at[me_d], tdst.at[me_d], send_td.at[o - 1], recv_td.at[me_d],
                 at_dst((me_d + o) % nd))
        c.start()
        pending.append(c)
    for o in range(1, nd):
        e = (me_d + o) % nd
        copy(tdst.at[e], tdst.at[e], send_td.at[o - 1], recv_td.at[e], at_dst(e)).wait_recv()
    tsrc[me_s] = sum(tdst[d] for d in range(nd))
    for o in range(1, ns):
        c = copy(tsrc.at[me_s], tsrc.at[me_s], send_ts.at[o - 1], recv_ts.at[me_s],
                 at_src((me_s + o) % ns))
        c.start()
        pending.append(c)
    for o in range(1, ns):
        e = (me_s + o) % ns
        copy(tsrc.at[e], tsrc.at[e], send_ts.at[o - 1], recv_ts.at[e], at_src(e)).wait_recv()
    whole = sum(tsrc[s] for s in range(ns))
    norm = jnp.sum(whole, axis=1, keepdims=True) / total_states
    norm = jnp.broadcast_to(norm, (2 * seqs, blk))
    scales[...] = norm
    inverse = 1.0 / norm

    def count(m, carry):
        r, c = table[3 * slots + m], table[4 * slots + m]
        left = jnp.concatenate([fwds[k][r // local, r % local] for k in range(2)], axis=0)
        right = jnp.concatenate([msgs[k][c // local, c % local] for k in range(2)], axis=0)
        right = (right.astype(jnp.float32) * inverse).astype(jnp.bfloat16)
        value = lax.dot_general(left, right, (((0,), (0,)), ((), ())),
                                preferred_element_type=jnp.float32)
        counts[m] = (value * trans[m].astype(jnp.float32) * table[5 * slots + m].astype(jnp.float32)).astype(jnp.bfloat16)
        return carry

    lax.fori_loop(0, slots, count, 0, unroll=4)

    def last_beta(a, raw):
        beta[a] = raw * inverse[seqs:]

    reduce_end(1, last_beta)
    for c in pending:
        c.wait_send()


def body(nd, ns, transitions, row_block, col_block, beta_last, emissions, forward):
    seqs, local, _, blk = beta_last.shape
    slots = transitions.shape[0]
    columns, rows = local * ns, local * nd
    total_states = rows * ns * blk

    live = row_block >= 0
    row = jnp.where(live, row_block // ns, 0)
    col = jnp.where(live, col_block % columns, 0)
    col = col % ns * local + col // ns
    key = jnp.where(live, row, rows)
    number = jnp.arange(slots)
    before = (key[None, :] < key[:, None]) | (
        (key[None, :] == key[:, None]) & (number[None, :] < number[:, None]))
    rank = jnp.sum(before.astype(jnp.int32), axis=1)
    place = (rank[None, :] == number[:, None]).astype(jnp.int32)
    perm = jnp.sum(place * number[None, :].astype(jnp.int32), axis=1)
    pcol = jnp.sum(place * col[None, :], axis=1)
    same = jnp.any((key[None, :] == key[:, None]) & (rank[None, :] == rank[:, None] - 1), axis=1)
    flag = jnp.sum(place * same[None, :].astype(jnp.int32), axis=1)
    every = jnp.arange(rows)
    prow = jnp.sum(place * row[None, :], axis=1)
    plive = jnp.sum(place * live[None, :].astype(jnp.int32), axis=1)
    last = jnp.where(jnp.any(key[None, :] == every[:, None], axis=1),
                     jnp.sum((key[None, :] <= every[:, None]).astype(jnp.int32), axis=1), 0)

    table = jnp.concatenate(
        [perm, pcol, flag, row, col, live.astype(jnp.int32), prow, plive, last]).astype(jnp.int32)

    lines = -(-rows // 128)
    last2 = jnp.pad(last.astype(jnp.int32), (0, lines * 128 - rows)).reshape(lines, 128)

    def by_block(array):
        return jnp.swapaxes(array[..., 0, :], -3, -2)

    msg0 = by_block((emissions[0].astype(jnp.float32) * beta_last).astype(jnp.bfloat16))
    em1 = by_block(emissions[1])
    fwd = by_block(forward)

    smem = pl.BlockSpec(memory_space=pltpu.SMEM)
    vmem = pl.BlockSpec(memory_space=pltpu.VMEM)
    nz, nx = nd // 2, ns // 2
    block = (local, seqs, blk)
    dma = pltpu.SemaphoreType.DMA
    counts, beta, scales = pl.pallas_call(
        functools.partial(kernel, nd, ns, float(total_states)),
        out_shape=(
            jax.ShapeDtypeStruct(transitions.shape, jnp.bfloat16),
            jax.ShapeDtypeStruct(block, jnp.float32),
            jax.ShapeDtypeStruct((2 * seqs, blk), jnp.float32),
        ),
        in_specs=[smem] + [vmem] * 5,
        out_specs=(vmem, vmem, vmem),
        scratch_shapes=[
            pltpu.VMEM((ns,) + block, jnp.bfloat16),
            pltpu.VMEM((ns,) + block, jnp.bfloat16),
            pltpu.VMEM((nd,) + block, jnp.bfloat16),
            pltpu.VMEM((nd,) + block, jnp.bfloat16),
            pltpu.VMEM((slots, seqs, blk), jnp.float32),
            pltpu.VMEM((slots, seqs, blk), jnp.float32),
            pltpu.VMEM((slots + 1, seqs, blk), jnp.bfloat16),
            pltpu.VMEM((slots + 1, seqs, blk), jnp.bfloat16),
            pltpu.VMEM((slots + 1, seqs, blk), jnp.bfloat16),
            pltpu.VMEM((slots + 1, seqs, blk), jnp.bfloat16),
            pltpu.VMEM((lines, 128), jnp.int32),
            pltpu.SMEM((lines, 128), jnp.int32),
            pltpu.VMEM((2, nz) + block, jnp.bfloat16),
            pltpu.VMEM((2, nz) + block, jnp.bfloat16),
            pltpu.VMEM((nd, 2 * seqs, blk), jnp.float32),
            pltpu.VMEM((ns, 2 * seqs, blk), jnp.float32),
            dma((2, 2 * nx)), dma((2, ns)),
            dma((2, 2 * nz)), dma((2, nd)),
            dma((2, 4)), dma((2, 4)),
            dma((2, nz)), dma((2, nz)),
            dma((nd,)), dma((nd,)),
            dma((ns,)), dma((ns,)),
            dma, dma, dma,
        ],
        compiler_params=pltpu.CompilerParams(
            collective_id=0, has_side_effects=True, vmem_limit_bytes=48 * 1024 * 1024),
    )(table, last2, transitions, msg0, em1, fwd)
    first, second = scales[:seqs, 0], scales[seqs:, 0]
    logs = jnp.log(jnp.stack([first, second / first]))
    return counts, jnp.swapaxes(beta, 0, 1)[:, :, None, :], logs


def solution(mesh):
    return jax.shard_map(
        functools.partial(body, mesh.shape["dst"], mesh.shape["src"]),
        mesh=mesh,
        in_specs=(
            P(("dst", "src"), None, None),
            P(("dst", "src")),
            P(("dst", "src")),
            P(None, "dst", "src", None),
            P(None, None, "dst", "src", None),
            P(None, None, "dst", "src", None),
        ),
        out_specs=(P(("dst", "src"), None, None), P(None, "dst", "src", None), P()),
        check_vma=False,
    )
```

```python
import functools

import jax
import jax.numpy as jnp
from jax import lax
from jax.experimental import pallas as pl
from jax.experimental.pallas import tpu as pltpu
from jax.sharding import PartitionSpec as P

MESH = pl.DeviceIdType.MESH


def kernel(nd, ns, total_states, table,
           trans, beta_in, emitted, fwd, counts, beta, scales,
           msgs0, msgs1, fwds0, fwds1, run, parts, ypart, zsend, zpart, tdst, tsrc,
           send_m, recv_m, send_f, recv_f, send_y, recv_y, send_z, recv_z,
           send_td, recv_td, send_ts, recv_ts):
    local, seqs, blk = beta_in.shape
    slots = trans.shape[0]
    nz, nx = nd // 2, ns // 2
    me_d, me_s = lax.axis_index("dst"), lax.axis_index("src")
    z, y = me_d // 2, me_d % 2
    x, core = me_s // 2, me_s % 2

    def at_dst(d):
        return (d, me_s)

    def at_src(s):
        return (me_d, s)

    def copy(src, dst, ssem, rsem, dev):
        return pltpu.make_async_remote_copy(
            src_ref=src, dst_ref=dst, send_sem=ssem, recv_sem=rsem,
            device_id=dev, device_id_type=MESH)

    barrier = pltpu.get_barrier_semaphore()
    for o in range(1, nd):
        pl.semaphore_signal(barrier, inc=1, device_id=at_dst((me_d + o) % nd), device_id_type=MESH)
    for o in range(1, ns):
        pl.semaphore_signal(barrier, inc=1, device_id=at_src((me_s + o) % ns), device_id_type=MESH)
    pl.semaphore_wait(barrier, nd + ns - 2)

    msgs, fwds = (msgs0, msgs1), (fwds0, fwds1)
    pending = []

    def other(pos, o):
        for bit in range(o.bit_length()):
            if o >> bit & 1:
                pos = pos + (1 << bit) - 2 * (pos // (1 << bit) % 2) * (1 << bit)
        return pos

    def gather_side(buf, k, me, side_dev, ssem, rsem):
        c = copy(buf[k].at[me], buf[k].at[me], ssem.at[k, 0], rsem.at[k, me], side_dev)
        c.start()
        pending.append(c)

    def gather_line(buf, k, me, count, dev, ssem, rsem):
        pos, side = me // 2, me % 2
        for o in range(1, count):
            c = copy(buf[k].at[me], buf[k].at[me], ssem.at[k, o], rsem.at[k, me],
                     dev(other(pos, o) * 2 + side))
            c.start()
            pending.append(c)

    def gather_pass(buf, k, me, offsets, count, side_dev, ssem, rsem):
        pos, side = me // 2, me % 2
        for o in offsets:
            e = other(pos, o) * 2 + side
            c = copy(buf[k].at[e], buf[k].at[e], ssem.at[k, count + o - 1], rsem.at[k, e], side_dev)
            c.wait_recv()
            c.start()
            pending.append(c)

    def gather_end(buf, k, me, count, side_dev, ssem, rsem):
        pos, side = me // 2, me % 2
        for o in range(count):
            e = other(pos, o) * 2 + 1 - side
            copy(buf[k].at[e], buf[k].at[e], ssem.at[k, 0], rsem.at[k, e], side_dev).wait_recv()

    mate_d = at_dst(z * 2 + 1 - y)
    mate_s = at_src(x * 2 + 1 - core)

    def message_gather(k):
        gather_line(msgs, k, me_s, nx, at_src, send_m, recv_m)
        gather_side(msgs, k, me_s, mate_s, send_m, recv_m)

    def message_arrive(k):
        gather_pass(msgs, k, me_s, range(1, nx), nx, mate_s, send_m, recv_m)
        gather_end(msgs, k, me_s, nx, mate_s, send_m, recv_m)

    def forward_pass(k, offsets):
        gather_pass(fwds, k, me_d, offsets, nz, mate_d, send_f, recv_f)

    def products(k):
        run[0] = jnp.zeros((seqs, blk), jnp.float32)

        def one(j, carry):
            c = table[slots + j]
            block = msgs[k][c // local, c % local]
            run[j + 1] = lax.dot_general(block, trans[table[j]], (((1,), (1,)), ((), ())),
                                         preferred_element_type=jnp.float32)
            return carry

        lax.fori_loop(0, slots, one, 0, unroll=8)

        def add_run(j, acc):
            acc = run[j + 1] + acc * table[2 * slots + j].astype(jnp.float32)
            run[j + 1] = acc
            return acc

        lax.fori_loop(0, slots, add_run, jnp.zeros((seqs, blk), jnp.float32), unroll=4)

        def put(r, carry):
            parts[k, r // local, r % local] = run[table[6 * slots + r]].astype(jnp.bfloat16)
            return carry

        lax.fori_loop(0, nd * local, put, 0, unroll=8)

    def reduce_side(k):
        for o in reversed(range(nz)):
            zt = other(z, o)
            c = copy(parts.at[k, zt * 2 + 1 - y], ypart.at[k, zt], send_y.at[k, o],
                     recv_y.at[k, zt], mate_d)
            c.start()
            pending.append(c)

    def reduce_line(k):
        for o in reversed(range(1, nz)):
            zt = other(z, o)
            copy(parts.at[k, zt * 2 + 1 - y], ypart.at[k, zt], send_y.at[k, o],
                 recv_y.at[k, zt], mate_d).wait_recv()

            def add(a, carry):
                zsend[k, zt, a] = (parts[k, zt * 2 + y, a].astype(jnp.float32)
                                   + ypart[k, zt, a].astype(jnp.float32)).astype(jnp.bfloat16)
                return carry

            lax.fori_loop(0, local, add, 0, unroll=4)
            c = copy(zsend.at[k, zt], zpart.at[k, z], send_z.at[k, o - 1], recv_z.at[k, z],
                     at_dst(zt * 2 + y))
            c.start()
            pending.append(c)

    def reduce_end(k):
        copy(parts.at[k, z * 2 + 1 - y], ypart.at[k, z], send_y.at[k, 0],
             recv_y.at[k, z], mate_d).wait_recv()
        for o in range(1, nz):
            zf = other(z, o)
            copy(zsend.at[k, zf], zpart.at[k, zf], send_z.at[k, o - 1], recv_z.at[k, zf],
                 mate_d).wait_recv()

        def add(a, total):
            raw = parts[k, me_d, a].astype(jnp.float32) + ypart[k, z, a].astype(jnp.float32)
            for o in range(1, nz):
                raw = raw + zpart[k, other(z, o), a].astype(jnp.float32)
            beta[a] = raw
            if k == 0:
                msgs[1][me_s, a] = (emitted[1, a].astype(jnp.float32) * raw).astype(jnp.bfloat16)
            return total + fwd[k, a].astype(jnp.float32) * raw

        total = lax.fori_loop(0, local, add, jnp.zeros((seqs, blk), jnp.float32), unroll=2)
        tdst[me_d, pl.ds(k * seqs, seqs)] = total

    def keep_message(a, carry):
        msgs[0][me_s, a] = (emitted[0, a].astype(jnp.float32) * beta_in[a]).astype(jnp.bfloat16)
        return carry

    lax.fori_loop(0, local, keep_message, 0, unroll=4)
    message_gather(0)
    for k in range(2):
        def keep_forward(a, carry, k=k):
            fwds[k][me_d, a] = fwd[k, a]
            return carry

        lax.fori_loop(0, local, keep_forward, 0, unroll=4)
    gather_line(fwds, 0, me_d, nz, at_dst, send_f, recv_f)
    gather_side(fwds, 0, me_d, mate_d, send_f, recv_f)
    message_arrive(0)
    forward_pass(0, range(1, 2))
    products(0)
    reduce_side(0)
    reduce_line(0)
    forward_pass(0, range(2, nz))
    gather_side(fwds, 1, me_d, mate_d, send_f, recv_f)
    gather_line(fwds, 1, me_d, nz, at_dst, send_f, recv_f)
    reduce_end(0)

    message_gather(1)
    message_arrive(1)
    forward_pass(1, range(1, 2))
    products(1)
    reduce_side(1)
    reduce_line(1)
    forward_pass(1, range(2, nz))
    reduce_end(1)

    for o in range(1, nd):
        c = copy(tdst.at[me_d], tdst.at[me_d], send_td.at[o - 1], recv_td.at[me_d],
                 at_dst((me_d + o) % nd))
        c.start()
        pending.append(c)
    for o in range(1, nd):
        e = (me_d + o) % nd
        copy(tdst.at[e], tdst.at[e], send_td.at[o - 1], recv_td.at[e], at_dst(e)).wait_recv()
    tsrc[me_s] = sum(tdst[d] for d in range(nd))
    for o in range(1, ns):
        c = copy(tsrc.at[me_s], tsrc.at[me_s], send_ts.at[o - 1], recv_ts.at[me_s],
                 at_src((me_s + o) % ns))
        c.start()
        pending.append(c)
    for o in range(1, ns):
        e = (me_s + o) % ns
        copy(tsrc.at[e], tsrc.at[e], send_ts.at[o - 1], recv_ts.at[e], at_src(e)).wait_recv()
    whole = sum(tsrc[s] for s in range(ns))
    norm = jnp.sum(whole, axis=1, keepdims=True) / total_states
    norm = jnp.broadcast_to(norm, (2 * seqs, blk))
    scales[...] = norm
    inverse = 1.0 / norm

    def finish(a, carry):
        beta[a] = beta[a] / norm[seqs:]
        return carry

    lax.fori_loop(0, local, finish, 0)

    for k in range(2):
        gather_end(fwds, k, me_d, nz, mate_d, send_f, recv_f)

    def count(m, carry):
        r, c = table[3 * slots + m], table[4 * slots + m]
        left = jnp.concatenate([fwds[k][r // local, r % local] for k in range(2)], axis=0)
        right = jnp.concatenate([msgs[k][c // local, c % local] for k in range(2)], axis=0)
        right = (right.astype(jnp.float32) * inverse).astype(jnp.bfloat16)
        value = lax.dot_general(left, right, (((0,), (0,)), ((), ())),
                                preferred_element_type=jnp.float32)
        counts[m] = (value * trans[m].astype(jnp.float32) * table[5 * slots + m].astype(jnp.float32)).astype(jnp.bfloat16)
        return carry

    lax.fori_loop(0, slots, count, 0, unroll=4)
    for c in pending:
        c.wait_send()


def body(nd, ns, transitions, row_block, col_block, beta_last, emissions, forward):
    seqs, local, _, blk = beta_last.shape
    slots = transitions.shape[0]
    columns, rows = local * ns, local * nd
    total_states = rows * ns * blk

    live = row_block >= 0
    row = jnp.where(live, row_block // ns, 0)
    col = jnp.where(live, col_block % columns, 0)
    col = col % ns * local + col // ns
    key = jnp.where(live, row, rows)
    number = jnp.arange(slots)
    before = (key[None, :] < key[:, None]) | (
        (key[None, :] == key[:, None]) & (number[None, :] < number[:, None]))
    rank = jnp.sum(before.astype(jnp.int32), axis=1)
    place = (rank[None, :] == number[:, None]).astype(jnp.int32)
    perm = jnp.sum(place * number[None, :].astype(jnp.int32), axis=1)
    pcol = jnp.sum(place * col[None, :], axis=1)
    same = jnp.any((key[None, :] == key[:, None]) & (rank[None, :] == rank[:, None] - 1), axis=1)
    flag = jnp.sum(place * same[None, :].astype(jnp.int32), axis=1)
    every = jnp.arange(rows)
    last = jnp.where(jnp.any(key[None, :] == every[:, None], axis=1),
                     jnp.sum((key[None, :] <= every[:, None]).astype(jnp.int32), axis=1), 0)

    table = jnp.concatenate(
        [perm, pcol, flag, row, col, live.astype(jnp.int32), last]).astype(jnp.int32)

    def by_block(array):
        return jnp.swapaxes(array[..., 0, :], -3, -2)

    beta_in = by_block(beta_last)
    emitted = by_block(emissions)
    fwd = by_block(forward)

    smem = pl.BlockSpec(memory_space=pltpu.SMEM)
    vmem = pl.BlockSpec(memory_space=pltpu.VMEM)
    nz, nx = nd // 2, ns // 2
    block = (local, seqs, blk)
    dma = pltpu.SemaphoreType.DMA
    counts, beta, scales = pl.pallas_call(
        functools.partial(kernel, nd, ns, float(total_states)),
        out_shape=(
            jax.ShapeDtypeStruct(transitions.shape, jnp.bfloat16),
            jax.ShapeDtypeStruct(block, jnp.float32),
            jax.ShapeDtypeStruct((2 * seqs, blk), jnp.float32),
        ),
        in_specs=[smem] + [vmem] * 4,
        out_specs=(vmem, vmem, vmem),
        scratch_shapes=[
            pltpu.VMEM((ns,) + block, jnp.bfloat16),
            pltpu.VMEM((ns,) + block, jnp.bfloat16),
            pltpu.VMEM((nd,) + block, jnp.bfloat16),
            pltpu.VMEM((nd,) + block, jnp.bfloat16),
            pltpu.VMEM((slots + 1, seqs, blk), jnp.float32),
            pltpu.VMEM((2, nd) + block, jnp.bfloat16),
            pltpu.VMEM((2, nz) + block, jnp.bfloat16),
            pltpu.VMEM((2, nz) + block, jnp.bfloat16),
            pltpu.VMEM((2, nz) + block, jnp.bfloat16),
            pltpu.VMEM((nd, 2 * seqs, blk), jnp.float32),
            pltpu.VMEM((ns, 2 * seqs, blk), jnp.float32),
            dma((2, 2 * nx)), dma((2, ns)),
            dma((2, 2 * nz)), dma((2, nd)),
            dma((2, nz)), dma((2, nz)),
            dma((2, nz)), dma((2, nz)),
            dma((nd,)), dma((nd,)),
            dma((ns,)), dma((ns,)),
        ],
        compiler_params=pltpu.CompilerParams(
            collective_id=0, has_side_effects=True, vmem_limit_bytes=48 * 1024 * 1024),
    )(table, transitions, beta_in, emitted, fwd)
    first, second = scales[:seqs, 0], scales[seqs:, 0]
    logs = jnp.log(jnp.stack([first, second / first]))
    return counts, jnp.swapaxes(beta, 0, 1)[:, :, None, :], logs


def solution(mesh):
    return jax.shard_map(
        functools.partial(body, mesh.shape["dst"], mesh.shape["src"]),
        mesh=mesh,
        in_specs=(
            P(("dst", "src"), None, None),
            P(("dst", "src")),
            P(("dst", "src")),
            P(None, "dst", "src", None),
            P(None, None, "dst", "src", None),
            P(None, None, "dst", "src", None),
        ),
        out_specs=(P(("dst", "src"), None, None), P(None, "dst", "src", None), P()),
        check_vma=False,
    )
```
